256 devices in a mesh: tm: 64 (over x, z, core), orb: 4 (over y).
Axes of the slice: x: 4, y: 4, z: 8, core: 2. Of those that a mesh axis runs over, the one named last changes fastest.
Arguments:
- history: bfloat16 [6, 64, 6, 64, 64, 128], P(None, None, None, 'tm', 'orb'), may hold values from -3 to 3
- hopping: bfloat16 [64, 64], replicated, may hold values from -0.75 to 0.75
- coupling: float32 [64], replicated, may hold values from 1 to 3
Outputs:
- row_one: bfloat16 [6, 64, 64, 128], P(None, 'tm', 'orb')
- corner_one: bfloat16 [64, 128], P('orb')
- row_two: bfloat16 [6, 64, 64, 128], P(None, 'tm', 'orb')
- edge_two: bfloat16 [64, 128], P('orb')
- corner_two: bfloat16 [64, 128], P('orb')
The draws below stay inside these ranges and needn't reach their ends.
All inputs are finite; a program needn't handle non-finite values.
Results may differ from the reference program's by a relative error of at most 0.0085.
The reference program's roundings to bfloat16 on the way count: a program that leaves them out, or rounds other values in their place, can miss the bound.
Values may be sent and summed in bfloat16 or wider, within the bound.
No kernel may reach another device: no remote copies, remote signals or barrier semaphores. Data moves between devices by JAX's collectives and lax.ppermute only.
A program may use at most 128 MiB of HBM per device.

```python
import math
import jax
import jax.numpy as jnp
from jax import lax

NORB = 64
ROUNDS = 6
OWNERS = 64


def block_scale(key, dims, split, low, top_value):
    def one(axis_at, blocks):
        steps = jax.random.uniform(jax.random.fold_in(jax.random.fold_in(key, 6), axis_at), (blocks,), jnp.float32, low / len(split), top_value / len(split))
        return jnp.repeat(jnp.exp(steps), dims[axis_at] // blocks).reshape((-1,) + (1,) * (len(dims) - axis_at - 1))

    gain = one(*split[0])
    for cut in split[1:]:
        gain = gain * one(*cut)
    return gain


def normal_values(own_key, dims, width, bound, cuts=(), kind=jnp.bfloat16):
    entries = jax.random.normal(own_key, dims, jnp.float32) * width
    if len(cuts) > 0:
        entries = block_scale(own_key, dims, cuts, -0.22, 0.18) * entries
    return jnp.clip(entries, min=-bound, max=bound).astype(kind)


def setup_inputs(seed: int = 0) -> dict:
    streams_of = jax.random.split(jax.random.key(seed), 4)
    history = normal_values(streams_of[0], (ROUNDS, OWNERS, ROUNDS, OWNERS, NORB, 2 * NORB), 0.5, 3.0, ((3, 64), (4, 4)))
    hopping = normal_values(streams_of[1], (NORB, NORB), NORB ** -0.5, 0.75)
    coupling = jnp.clip(jnp.exp(jax.random.uniform(streams_of[2], (NORB,), jnp.float32, math.log(1.0), math.log(3.0))), 1.0, 3.0)
    return {"history": history, "hopping": hopping, "coupling": coupling}


STEP = 0.08


def self_energy(blocks, row_gain, column_gain):
    orbitals = column_gain.shape[0]
    real_part = blocks[..., :orbitals].astype(jnp.float32)
    imag_part = blocks[..., orbitals:].astype(jnp.float32)
    strength = -(row_gain[:, None] * column_gain[None, :]) * (real_part * real_part + imag_part * imag_part)
    return jnp.concatenate([strength * real_part, strength * imag_part], axis=-1).astype(jnp.bfloat16)


def combine(first, second, orbitals):
    return jnp.concatenate([first[..., :orbitals] - second[..., orbitals:], first[..., orbitals:] + second[..., :orbitals]], axis=-1)


def advance(older, change, orbitals):
    older = older.astype(jnp.float32)
    return jnp.concatenate([older[..., :orbitals] + STEP * change[..., orbitals:], older[..., orbitals:] - STEP * change[..., :orbitals]], axis=-1)


def hermitian(whole, orbitals):
    real_part = whole[:, :orbitals]
    imag_part = whole[:, orbitals:]
    return jnp.concatenate([real_part + real_part.T, imag_part - imag_part.T], axis=-1)


def reference(history, hopping, coupling):
    orbitals = hopping.shape[0]
    times = ROUNDS * OWNERS
    grid = history.reshape(times, times, orbitals, 2 * orbitals)
    turned = hopping.T

    def apply_hop(blocks):
        return jnp.concatenate([jnp.dot(blocks[..., :orbitals], turned, preferred_element_type=jnp.float32), jnp.dot(blocks[..., orbitals:], turned, preferred_element_type=jnp.float32)], axis=-1)

    order = jnp.arange(times, dtype=jnp.int32)

    def collide(sigma):
        factor = sigma.astype(jnp.float32)

        def column_term(target):
            blocks = lax.dynamic_index_in_dim(grid, target, 1, keepdims=False)
            keep = (order <= target)[:, None, None]
            blocks = jnp.where(keep, blocks, jnp.zeros_like(blocks)).astype(jnp.float32)
            first = jnp.einsum("sjk,ski->ji", blocks[..., :orbitals], factor)
            second = jnp.einsum("sjk,ski->ji", blocks[..., orbitals:], factor)
            return combine(first, second, orbitals)

        return lax.map(column_term, order)

    last_row = grid[times - 1]
    sigma = self_energy(last_row, coupling, coupling)
    change = apply_hop(last_row) + STEP * collide(sigma)
    row_one = advance(last_row, change, orbitals).astype(jnp.bfloat16)
    corner_one = advance(last_row[times - 1], hermitian(change[times - 1], orbitals), orbitals).astype(jnp.bfloat16)

    sigma_two = self_energy(row_one, coupling, coupling)
    corner_sigma = self_energy(corner_one, coupling, coupling)
    corner_factor = corner_sigma.astype(jnp.float32)
    row_factor = row_one.astype(jnp.float32)
    instant = combine(jnp.einsum("tjk,ki->tji", row_factor[..., :orbitals], corner_factor), jnp.einsum("tjk,ki->tji", row_factor[..., orbitals:], corner_factor), orbitals)
    change_two = apply_hop(row_one) + instant + STEP * collide(sigma_two)
    row_two = advance(row_one, change_two, orbitals).astype(jnp.bfloat16)

    factor = sigma_two.astype(jnp.float32)
    first = -jnp.einsum("skj,ski->ji", row_one[..., :orbitals].astype(jnp.float32), factor)
    second = jnp.einsum("skj,ski->ji", row_one[..., orbitals:].astype(jnp.float32), factor)
    column = combine(first, second, orbitals)
    own = combine(jnp.dot(corner_one[:, :orbitals], corner_sigma, preferred_element_type=jnp.float32), jnp.dot(corner_one[:, orbitals:], corner_sigma, preferred_element_type=jnp.float32), orbitals)
    change_edge = apply_hop(corner_one) + STEP * (column + own)
    edge_two = advance(corner_one, change_edge, orbitals).astype(jnp.bfloat16)
    corner_two = advance(corner_one, hermitian(change_edge, orbitals), orbitals).astype(jnp.bfloat16)
    shape = (ROUNDS, OWNERS, orbitals, 2 * orbitals)
    return (row_one.reshape(shape), corner_one, row_two.reshape(shape), edge_two, corner_two)
```

```python
import functools

import jax
import jax.numpy as jnp
from jax import lax
from jax.experimental import pallas as pl
from jax.experimental.pallas import tpu as pltpu
from jax.sharding import Mesh, PartitionSpec as P

STEP = 0.08
XS, ZS, CORES, YS = 4, 8, 2, 4
ROUNDS = 6
HALF = ROUNDS // 2
ORB = 64
ROWS = ORB // YS
WIDE = 2 * ORB
COLS = ROUNDS * ROWS
GROUP = ZS * HALF
SHIFTS = (1, 3, 2)


def ring(size, distance):
    return [(i, (i + distance) % size) for i in range(size)]


def swap_cores(array):
    return lax.ppermute(array, "core", [(0, 1), (1, 0)])


def around(array, axis):
    pieces = {0: array}
    for distance in SHIFTS:
        pieces[distance] = lax.ppermute(array, axis, ring(4, distance))
    return [pieces[d] for d in range(4)]


def self_energy(blocks, row_gain, column_gain):
    real_part = blocks[..., :ORB].astype(jnp.float32)
    imag_part = blocks[..., ORB:].astype(jnp.float32)
    strength = -(row_gain[:, None] * column_gain[None, :]) * (
        real_part * real_part + imag_part * imag_part
    )
    return jnp.concatenate([strength * real_part, strength * imag_part], axis=-1).astype(
        jnp.bfloat16
    )


def combine(first, second):
    return jnp.concatenate(
        [
            first[..., :ORB] - second[..., ORB:],
            first[..., ORB:] + second[..., :ORB],
        ],
        axis=-1,
    )


def advance(older, change):
    older = older.astype(jnp.float32)
    return jnp.concatenate(
        [
            older[..., :ORB] + STEP * change[..., ORB:],
            older[..., ORB:] - STEP * change[..., :ORB],
        ],
        axis=-1,
    )


def hermitian(whole):
    real_part = whole[:, :ORB]
    imag_part = whole[:, ORB:]
    return jnp.concatenate([real_part + real_part.T, imag_part - imag_part.T], axis=-1)


def times_i(slab):
    return jnp.concatenate([-slab[:, ORB:], slab[:, :ORB]], axis=-1)


def collide_kernel(place, own, other, a0, a1, a2, a3, b0, b1, b2, b3, out, factor):
    step = pl.program_id(0)
    x, y, core, mine, partner = (place[i] for i in range(5))
    source = lax.rem(x - step + XS, XS)

    def put(round_at, z, dy, slab):
        row = pl.multiple_of(lax.rem(y - dy + YS, YS) * ROWS, ROWS)
        factor[round_at, pl.ds(z * WIDE + row, ROWS), :] = slab
        factor[round_at, pl.ds(z * WIDE + ORB + row, ROWS), :] = times_i(slab)

    for dx, block in enumerate((a0, a1, a2, a3)):

        @pl.when(step == dx)
        def _(block=block):
            for dy in range(YS):
                for z in range(ZS):
                    for r in range(HALF):
                        put(r, z, dy, block[dy * GROUP + z * HALF + r])

    for dy, block in enumerate((b0, b1, b2, b3)):
        for z in range(ZS):
            for r in range(HALF):
                put(HALF + r, z, dy, block[step * GROUP + z * HALF + r])

    @pl.when(step == 0)
    def _():
        out[...] = jnp.zeros_like(out)

    for a in range(ROUNDS):
        low = a * ROWS
        count = COLS - low
        sides = []
        for table, target in ((own, mine), (other, partner)):
            pieces = []
            for z in range(ZS):
                block = table[a, 0, z, 0, low:, :]
                time = (source * ZS + z) * CORES + core
                first = jnp.where(time <= target, block[:ROWS], jnp.zeros_like(block[:ROWS]))
                if count > ROWS:
                    block = jnp.concatenate([first, block[ROWS:]], axis=0)
                else:
                    block = first
                pieces.append(block)
            sides.append(jnp.concatenate(pieces, axis=1))
        product = jnp.dot(
            jnp.concatenate(sides, axis=0), factor[a], preferred_element_type=jnp.float32
        )
        out[0, low:, :] += product[:count]
        out[1, low:, :] += product[count:]


def collide(place, own, other, first, second):
    whole = [pl.BlockSpec(a.shape, lambda i, p: (0, 0, 0)) for a in first + second]
    return pl.pallas_call(
        collide_kernel,
        grid_spec=pltpu.PrefetchScalarGridSpec(
            num_scalar_prefetch=1,
            grid=(XS,),
            in_specs=[
                pl.BlockSpec(
                    (ROUNDS, 1, ZS, 1, COLS, WIDE),
                    lambda i, p: (0, lax.rem(p[0] - i + XS, XS), 0, p[2], 0, 0),
                ),
                pl.BlockSpec(
                    (ROUNDS, 1, ZS, 1, COLS, WIDE),
                    lambda i, p: (0, lax.rem(p[0] - i + XS, XS), 0, 0, 0, 0),
                ),
            ]
            + whole,
            out_specs=pl.BlockSpec((2, COLS, WIDE), lambda i, p: (0, 0, 0)),
            scratch_shapes=[pltpu.VMEM((ROUNDS, ZS * WIDE, WIDE), jnp.bfloat16)],
        ),
        out_shape=jax.ShapeDtypeStruct((2, COLS, WIDE), jnp.float32),
        compiler_params=pltpu.CompilerParams(vmem_limit_bytes=40 * 1024 * 1024),
        name="collide",
    )(place, own, other, *first, *second)


def split(value):
    high = lax.reduce_precision(value, 8, 7)
    return high.astype(jnp.bfloat16), (value - high).astype(jnp.bfloat16)


def body(history, hopping, coupling):
    x, z = lax.axis_index("x"), lax.axis_index("z")
    core, y = lax.axis_index("core"), lax.axis_index("orb")
    owner = (x * ZS + z) * CORES + core
    place = jnp.stack([x, y, core, owner, owner + 1 - 2 * core]).astype(jnp.int32)
    table = history.reshape(ROUNDS, XS, ZS, CORES, COLS, WIDE)
    partner = swap_cores(
        lax.dynamic_slice_in_dim(table, 1 - core, 1, axis=3)
    )
    row_gain = lax.dynamic_slice_in_dim(coupling, y * ROWS, ROWS)
    turned = hopping.T

    def apply_hop(blocks):
        return jnp.concatenate(
            [
                jnp.dot(blocks[..., :ORB], turned, preferred_element_type=jnp.float32),
                jnp.dot(blocks[..., ORB:], turned, preferred_element_type=jnp.float32),
            ],
            axis=-1,
        )

    def own_rows(whole):
        return lax.dynamic_slice_in_dim(whole, y * ROWS, ROWS, 0)

    def in_order(pieces):
        twice = jnp.stack([pieces[d] for d in (3, 2, 1, 0, 3, 2, 1)])
        return lax.dynamic_slice_in_dim(twice, 3 - y, 4, 0)

    def over_z(payload):
        return lax.all_to_all(jnp.broadcast_to(payload[None], (ZS,) + payload.shape), "z", 0, 0)

    def finish(parts):
        return (parts[0] + swap_cores(parts[1])).reshape(ROUNDS, ROWS, WIDE)

    last_row = history[ROUNDS - 1, XS * ZS * CORES - 1, :, 0]

    sigma = self_energy(last_row, row_gain, coupling)
    planes = over_z(sigma)
    first = around(planes[:, :HALF].reshape(GROUP, ROWS, WIDE), "orb")
    second = around(planes[:, HALF:].reshape(GROUP, ROWS, WIDE), "x")
    first = around(jnp.concatenate(first), "x")
    second = around(jnp.concatenate(second), "orb")
    change = apply_hop(last_row) + STEP * finish(collide(place, table, partner, first, second))
    row_one = advance(last_row, change).astype(jnp.bfloat16)
    sigma_two = self_energy(row_one, row_gain, coupling)

    overlap = jnp.einsum(
        "skj,ski->ji", row_one, sigma_two, preferred_element_type=jnp.float32
    )
    partial = combine(-overlap[:ORB], overlap[ORB:])
    column = own_rows(partial)
    for distance in SHIFTS:
        slab = lax.dynamic_slice_in_dim(partial, lax.rem(y + distance, YS) * ROWS, ROWS, 0)
        column = column + lax.ppermute(slab, "orb", ring(4, distance))

    last = ROUNDS - 1
    payload = jnp.concatenate([sigma_two, jnp.stack(split(change[last]) + (last_row[last],))])
    planes = over_z(payload)
    riders = planes[ZS - 1, ROUNDS:]
    first = around(
        jnp.concatenate([planes[:, :HALF].reshape(GROUP, ROWS, WIDE), riders]), "orb"
    )
    second = around(
        jnp.concatenate(
            [planes[:, HALF:ROUNDS].reshape(GROUP, ROWS, WIDE), jnp.stack(split(column))]
        ),
        "x",
    )
    riders = in_order([piece[GROUP:] for piece in first])
    newest = (riders[:, 0].astype(jnp.float32) + riders[:, 1].astype(jnp.float32)).reshape(
        ORB, WIDE
    )
    corner = advance(riders[:, 2].reshape(ORB, WIDE), hermitian(newest)).astype(jnp.bfloat16)
    column = sum(
        piece[GROUP].astype(jnp.float32) + piece[GROUP + 1].astype(jnp.float32)
        for piece in second
    )
    first = around(
        jnp.concatenate(
            [piece[:GROUP] for piece in first] + [corner.reshape(YS, ROWS, WIDE)]
        ),
        "x",
    )
    second = around(jnp.concatenate([piece[:GROUP] for piece in second]), "orb")
    column = jnp.sum(
        lax.all_to_all(
            jnp.broadcast_to(column[None], (ZS * CORES,) + column.shape), ("z", "core"), 0, 0
        ),
        axis=0,
    )
    column = in_order(around(column, "orb")).reshape(ORB, WIDE)
    from_last = lax.rem(x + 1, XS)
    corner = sum(
        jnp.where(from_last == d, first[d][4 * GROUP :], jnp.zeros((), jnp.bfloat16))
        for d in range(XS)
    )
    corner = jnp.where(core == 1, corner, swap_cores(corner)).reshape(ORB, WIDE)
    corner_sigma = self_energy(corner, coupling, coupling)

    def times_corner(blocks):
        return combine(
            jnp.dot(blocks[..., :ORB], corner_sigma, preferred_element_type=jnp.float32),
            jnp.dot(blocks[..., ORB:], corner_sigma, preferred_element_type=jnp.float32),
        )

    totals = finish(collide(place, table, partner, first, second))
    change_two = apply_hop(row_one) + times_corner(row_one) + STEP * totals
    row_two = advance(row_one, change_two).astype(jnp.bfloat16)
    edge_change = apply_hop(corner) + STEP * (column + times_corner(corner))
    edge_two = own_rows(advance(corner, edge_change)).astype(jnp.bfloat16)
    corner_two = own_rows(advance(corner, hermitian(edge_change))).astype(jnp.bfloat16)
    shape = (ROUNDS, 1, ROWS, WIDE)
    return (
        row_one.reshape(shape),
        own_rows(corner),
        row_two.reshape(shape),
        edge_two,
        corner_two,
    )


def solution(mesh):
    fine = Mesh(mesh.devices.reshape(XS, ZS, CORES, YS), ("x", "z", "core", "orb"))
    tm = ("x", "z", "core")
    return jax.shard_map(
        body,
        mesh=fine,
        in_specs=(P(None, None, None, tm, "orb", None), P(), P()),
        out_specs=(
            P(None, tm, "orb", None),
            P("orb", None),
            P(None, tm, "orb", None),
            P("orb", None),
            P("orb", None),
        ),
        check_vma=False,
    )
```

```python
import jax
import jax.numpy as jnp
from jax import lax
from jax.experimental import pallas as pl
from jax.experimental.pallas import tpu as pltpu
from jax.sharding import Mesh, PartitionSpec as P

STEP = 0.08
XS, ZS, CORES, YS = 4, 8, 2, 4
ROUNDS = 6
ORB = 64
ROWS = ORB // YS
WIDE = 2 * ORB
COLS = ROUNDS * ROWS
TIMES = ROUNDS * XS * ZS * CORES
EXTRA = 3
HALF = ROUNDS // 2
DEEP = 2
STEPS = ZS // DEEP
GROUP = ZS * HALF


def swap_cores(array):
    return lax.ppermute(array, "core", [(0, 1), (1, 0)])


def around(array, axis):
    pieces = {0: array}
    for distance in (1, 3, 2):
        pairs = [(i, (i + distance) % 4) for i in range(4)]
        pieces[distance] = lax.ppermute(array, axis, pairs)
    return [pieces[d] for d in range(4)]


def halves_swapped(value):
    return jnp.concatenate([value[:, ORB:], value[:, :ORB]], axis=-1)


def times_i(value):
    return jnp.concatenate([-value[:, ORB:], value[:, :ORB]], axis=-1)


def matrix_of(value):
    return jnp.concatenate([value, times_i(value)], axis=0)


def stepped(older, change):
    return older.astype(jnp.float32) - STEP * times_i(change)


def self_energy(blocks, gain):
    parts = blocks.astype(jnp.float32)
    square = parts * parts
    return (gain * (square + halves_swapped(square)) * parts).astype(jnp.bfloat16)


def hermitian(whole):
    real_part = whole[:, :ORB]
    imag_part = whole[:, ORB:]
    return jnp.concatenate([real_part + real_part.T, imag_part - imag_part.T], axis=-1)


def head_kernel(place, last, column, row, payload, gain_out):
    pair = jnp.concatenate([row[...], row[...]], axis=1)
    gain = -(column[...] * pair)
    gain = jnp.concatenate([gain] * ROUNDS, axis=0)
    gain_out[...] = gain
    sigma = self_energy(last[0, 0], gain)
    for z in range(ZS):
        payload[z] = sigma


def head(place, rows_of, coupling):
    return pl.pallas_call(
        head_kernel,
        grid_spec=pltpu.PrefetchScalarGridSpec(
            num_scalar_prefetch=1,
            grid=(1,),
            in_specs=[
                pl.BlockSpec(
                    (1, 1, COLS, WIDE), lambda i, p: (ROUNDS - 1, TIMES // ROUNDS - 1, 0, 0)
                ),
                pl.BlockSpec((ROWS, 1), lambda i, p: (p[4], 0)),
                pl.BlockSpec((1, ORB), lambda i, p: (0, 0)),
            ],
            out_specs=[
                pl.BlockSpec((ZS, COLS, WIDE), lambda i, p: (0, 0, 0)),
                pl.BlockSpec((COLS, WIDE), lambda i, p: (0, 0)),
            ],
        ),
        out_shape=[
            jax.ShapeDtypeStruct((ZS, COLS, WIDE), jnp.bfloat16),
            jax.ShapeDtypeStruct((COLS, WIDE), jnp.float32),
        ],
        compiler_params=pltpu.CompilerParams(vmem_limit_bytes=56 * 1024 * 1024),
        name="head",
    )(place, rows_of, coupling.reshape(ORB, 1), coupling.reshape(1, ORB))


def collide_kernel(
    place, own, other, a0, a1, a2, a3, b0, b1, low_two, high_two, b3, out, total, factor
):
    step = pl.program_id(0)
    core, x, y = place[0], place[3], place[4]
    firsts = (a0, a1, a2, a3)
    sources = [lax.rem(x - dx + XS, XS) for dx in range(XS)]
    empty = jnp.zeros((ORB, WIDE), jnp.bfloat16)

    @pl.when(step == 0)
    def _():
        total[...] = jnp.zeros_like(total)
        factor[...] = jnp.zeros_like(factor)

    for dy in range(YS):
        row = pl.multiple_of(lax.rem(y - dy + YS, YS) * ROWS, ROWS)
        for dx in range(XS):
            if dy == 2:
                piece = (low_two, high_two)[dx // 2].at[dx % 2]
            else:
                piece = (b0, b1, None, b3)[dy].at[dx]
            for z in range(DEEP):
                base = (dx * DEEP + z) * WIDE
                for r in range(HALF):
                    slab = piece[z * HALF + r]
                    factor[r, pl.ds(base + row, ROWS), :WIDE] = slab
                    factor[r, pl.ds(base + ORB + row, ROWS), WIDE:] = slab

    for a in range(ROUNDS):
        low, count = a * ROWS, COLS - a * ROWS
        sides = []
        for table, target in ((own, place[1]), (other, place[2])):
            blocks = []
            for dx in range(XS):
                for z in range(DEEP):
                    block = table[a, sources[dx], z, 0, low:, :]
                    time = (sources[dx] * ZS + step * DEEP + z) * CORES + core
                    diagonal = jnp.where(
                        time <= target, block[:ROWS], jnp.zeros_like(block[:ROWS])
                    )
                    if count > ROWS:
                        diagonal = jnp.concatenate([diagonal, block[ROWS:]], axis=0)
                    blocks.append(diagonal)
            sides.append(jnp.concatenate(blocks, axis=1))
        if a < HALF:
            blocks = []
            for dx in range(XS):
                for z in range(DEEP):
                    block = jnp.concatenate(
                        [
                            firsts[dx][lax.rem(y - i + YS, YS), z * HALF + a]
                            for i in range(YS)
                        ],
                        axis=0,
                    )
                    blocks.append(jnp.concatenate([block, empty], axis=1))
                    blocks.append(jnp.concatenate([empty, block], axis=1))
            right = jnp.concatenate(blocks, axis=0)
        else:
            right = factor[a - HALF]
        product = jnp.dot(
            jnp.concatenate(sides, axis=0), right, preferred_element_type=jnp.float32
        )
        total[0, low:, :] += product[:count]
        total[1, low:, :] += product[count:]

    @pl.when(step == STEPS - 1)
    def _():
        for side in range(2):
            out[side] = total[side, :, :WIDE] + times_i(total[side, :, WIDE:])


def collide(place, own, other, first, second):
    half = pl.BlockSpec(
        (ROUNDS, XS, DEEP, 1, COLS, WIDE), lambda i, p: (0, 0, i, p[0], 0, 0)
    )
    pieces = first + second
    slabs = [
        pl.BlockSpec((piece.shape[0], DEEP * HALF, ROWS, WIDE), lambda i, p: (0, i, 0, 0))
        for piece in pieces
    ]
    return pl.pallas_call(
        collide_kernel,
        grid_spec=pltpu.PrefetchScalarGridSpec(
            num_scalar_prefetch=1,
            grid=(STEPS,),
            in_specs=[half, half] + slabs,
            out_specs=pl.BlockSpec((2, COLS, WIDE), lambda i, p: (0, 0, 0)),
            scratch_shapes=[
                pltpu.VMEM((2, COLS, 2 * WIDE), jnp.float32),
                pltpu.VMEM((HALF, XS * DEEP * WIDE, 2 * WIDE), jnp.bfloat16),
            ],
        ),
        out_shape=jax.ShapeDtypeStruct((2, COLS, WIDE), jnp.float32),
        compiler_params=pltpu.CompilerParams(vmem_limit_bytes=48 * 1024 * 1024),
        name="collide",
    )(place, own, other, *pieces)


def pair(value):
    high = value.astype(jnp.bfloat16)
    return high, (value - high.astype(jnp.float32)).astype(jnp.bfloat16)


def joined(high, low):
    return high.astype(jnp.float32) + low.astype(jnp.float32)


def update_kernel(sums, theirs, last, hop, gain, row_out, payload):
    older = last[...]
    change = jnp.dot(older, hop[...], preferred_element_type=jnp.float32) + STEP * (
        sums[0] + theirs[...]
    )
    row = stepped(older, change).astype(jnp.bfloat16)
    sigma = self_energy(row, gain[...])
    row_out[...] = row
    overlap = lax.dot_general(
        row, sigma, (((0,), (0,)), ((), ())), preferred_element_type=jnp.float32
    )
    column = (times_i(overlap[ORB:]) - overlap[:ORB]).astype(jnp.bfloat16)
    riders = pair(change[COLS - ROWS :]) + (older[COLS - ROWS :], column)
    whole = jnp.concatenate((sigma,) + riders, axis=0)
    for z in range(ZS):
        payload[z] = whole


def update(sums, theirs, last, hop, gain):
    return pl.pallas_call(
        update_kernel,
        out_shape=[
            jax.ShapeDtypeStruct((COLS, WIDE), jnp.bfloat16),
            jax.ShapeDtypeStruct((ZS, COLS + EXTRA * ROWS + ORB, WIDE), jnp.bfloat16),
        ],
        name="update",
    )(sums, theirs, last, hop, gain)


def close_kernel(sums, theirs, row, hop, corner_factor, row_out):
    older = row[...]
    change = (
        jnp.dot(older, hop[...], preferred_element_type=jnp.float32)
        + jnp.dot(older, corner_factor[...], preferred_element_type=jnp.float32)
        + STEP * (sums[0] + theirs[...])
    )
    row_out[...] = stepped(older, change).astype(jnp.bfloat16)


def close(sums, theirs, row, hop, corner_factor):
    return pl.pallas_call(
        close_kernel,
        out_shape=jax.ShapeDtypeStruct((COLS, WIDE), jnp.bfloat16),
        name="close",
    )(sums, theirs, row, hop, corner_factor)


def body(history, hopping, coupling):
    x, z = lax.axis_index("x"), lax.axis_index("z")
    core, y = lax.axis_index("core"), lax.axis_index("orb")
    owner = (x * ZS + z) * CORES + core
    place = jnp.stack([core, owner, owner + 1 - 2 * core, x, y]).astype(jnp.int32)
    table = history.reshape(ROUNDS, XS, ZS, CORES, COLS, WIDE)
    rows_of = history.reshape(ROUNDS, TIMES // ROUNDS, COLS, WIDE)
    turned = hopping.T
    empty = jnp.zeros_like(turned)
    hop = jnp.concatenate(
        [
            jnp.concatenate([turned, empty], axis=1),
            jnp.concatenate([empty, turned], axis=1),
        ],
        axis=0,
    )
    corner_gain = -(coupling[:, None] * jnp.concatenate([coupling, coupling])[None, :])

    def own_rows(whole):
        return lax.dynamic_slice_in_dim(whole, y * ROWS, ROWS, 0)

    def along_both(first, second):
        first, second = lax.optimization_barrier((first, second))
        first, second = around(first, "orb"), around(second, "x")
        first, second = lax.optimization_barrier((first, second))
        first, second = jnp.concatenate(first), jnp.concatenate(second)
        first, second = lax.optimization_barrier((first, second))
        return along_again(first, second)

    def along_again(first, second):
        ahead = lax.ppermute(second, "orb", [(i, (i + 1) % YS) for i in range(YS)])
        behind = lax.ppermute(second, "orb", [(i, (i + 3) % YS) for i in range(YS)])
        middle = second.shape[0] // 2
        low = lax.ppermute(ahead[:middle], "orb", [(i, (i + 1) % YS) for i in range(YS)])
        high = lax.ppermute(behind[middle:], "orb", [(i, (i + 3) % YS) for i in range(YS)])
        first = [piece.reshape(YS, -1, ROWS, WIDE) for piece in around(first, "x")]
        second = [
            piece.reshape(-1, second.shape[0] // XS, ROWS, WIDE)
            for piece in (second, ahead, low, high, behind)
        ]
        return lax.optimization_barrier((first, second))

    def plane_parts(planes):
        parts = planes.reshape(ZS, -1, ROWS, WIDE)
        return (
            parts[:, :HALF].reshape(GROUP, ROWS, WIDE),
            parts[:, HALF:ROUNDS].reshape(GROUP, ROWS, WIDE),
        )

    def ring_sum(pieces):
        a, b, c, d = pieces
        return (a + c) + (b + d)

    other = swap_cores(table)
    payload, gains = head(place, rows_of, coupling)
    planes = lax.all_to_all(payload, "z", 0, 0)
    last_row = rows_of[ROUNDS - 1, TIMES // ROUNDS - 1]
    planes, other, last_row, hop, gains, corner_gain = lax.optimization_barrier(
        (planes, other, last_row, hop, gains, corner_gain)
    )
    first, second = along_both(*plane_parts(planes))
    sums = collide(place, table, other, first, second)
    row_one, payload = update(sums, swap_cores(sums[1]), last_row, hop, gains)

    planes = lax.all_to_all(payload, "z", 0, 0)
    first, second = plane_parts(planes)
    parts = planes.reshape(ZS, -1, ROWS, WIDE)
    riders = parts[ZS - 1, ROUNDS : ROUNDS + EXTRA]
    column = jnp.sum(parts[:, ROUNDS + EXTRA :].astype(jnp.float32), axis=0)
    first, second = along_both(
        jnp.concatenate([first, riders]),
        jnp.concatenate([second, column.astype(jnp.bfloat16)]),
    )
    from_last = lax.rem(x + 1, XS)
    riders = first[0][:, GROUP:]
    for d in range(1, XS):
        riders = jnp.where(from_last == d, first[d][:, GROUP:], riders)
    riders = jnp.stack([riders[d] for d in (3, 2, 1, 0, 3, 2, 1)])
    riders = lax.dynamic_slice_in_dim(riders, 3 - y, YS, 0)
    newest = joined(riders[:, 0], riders[:, 1]).reshape(ORB, WIDE)
    corner = stepped(riders[:, 2].reshape(ORB, WIDE), hermitian(newest)).astype(jnp.bfloat16)
    corner = jnp.where(core == 1, corner, swap_cores(corner))
    columns = [piece[:, GROUP:].astype(jnp.float32) for piece in second]
    columns = [columns[0], columns[1], jnp.concatenate(columns[2:4]), columns[4]]
    column = ring_sum([ring_sum(piece) for piece in columns]).reshape(ORB, WIDE)
    column = column + swap_cores(column)
    corner_factor = matrix_of(self_energy(corner, corner_gain))
    edge_change = jnp.dot(corner, hop, preferred_element_type=jnp.float32) + STEP * (
        column + jnp.dot(corner, corner_factor, preferred_element_type=jnp.float32)
    )
    edge_two = own_rows(stepped(corner, edge_change)).astype(jnp.bfloat16)
    corner_two = own_rows(stepped(corner, hermitian(edge_change))).astype(jnp.bfloat16)

    sums = collide(place, table, other, first, second)
    row_two = close(sums, swap_cores(sums[1]), row_one, hop, corner_factor)
    shape = (ROUNDS, 1, ROWS, WIDE)
    return (
        row_one.reshape(shape),
        own_rows(corner),
        row_two.reshape(shape),
        edge_two,
        corner_two,
    )


def solution(mesh):
    fine = Mesh(mesh.devices.reshape(XS, ZS, CORES, YS), ("x", "z", "core", "orb"))
    tm = ("x", "z", "core")
    return jax.shard_map(
        body,
        mesh=fine,
        in_specs=(P(None, None, None, tm, "orb", None), P(), P()),
        out_specs=(
            P(None, tm, "orb", None),
            P("orb", None),
            P(None, tm, "orb", None),
            P("orb", None),
            P("orb", None),
        ),
        check_vma=False,
    )
```

```python
import jax
import jax.numpy as jnp
from jax import lax
from jax.experimental import pallas as pl
from jax.experimental.pallas import tpu as pltpu
from jax.sharding import Mesh, PartitionSpec as P

STEP = 0.08
XS, ZS, CORES, YS = 4, 8, 2, 4
ROUNDS = 6
ORB = 64
ROWS = ORB // YS
WIDE = 2 * ORB
COLS = ROUNDS * ROWS
TIMES = ROUNDS * XS * ZS * CORES
EXTRA = 3
HALF = ROUNDS // 2
DEEP = 2
STEPS = ZS // DEEP
GROUP = ZS * HALF


def swap_cores(array):
    return lax.ppermute(array, "core", [(0, 1), (1, 0)])


def around(array, axis):
    pieces = {0: array}
    for distance in (1, 3, 2):
        pairs = [(i, (i + distance) % 4) for i in range(4)]
        pieces[distance] = lax.ppermute(array, axis, pairs)
    return [pieces[d] for d in range(4)]


def halves_swapped(value):
    return jnp.concatenate([value[:, ORB:], value[:, :ORB]], axis=-1)


def times_i(value):
    return jnp.concatenate([-value[:, ORB:], value[:, :ORB]], axis=-1)


def matrix_of(value):
    return jnp.concatenate([value, times_i(value)], axis=0)


def stepped(older, change):
    return older.astype(jnp.float32) - STEP * times_i(change)


def self_energy(blocks, gain):
    parts = blocks.astype(jnp.float32)
    square = parts * parts
    return (gain * (square + halves_swapped(square)) * parts).astype(jnp.bfloat16)


def hermitian(whole):
    real_part = whole[:, :ORB]
    imag_part = whole[:, ORB:]
    return jnp.concatenate([real_part + real_part.T, imag_part - imag_part.T], axis=-1)


def gain_of(row, first, count):
    lane = lax.broadcasted_iota(jnp.int32, (count, ORB), 1)
    line = lax.broadcasted_iota(jnp.int32, (count, ORB), 0)
    mine = jnp.where(lane == line + first, jnp.broadcast_to(row, (count, ORB)), 0.0)
    column = jnp.sum(mine, axis=1, keepdims=True)
    return -(column * jnp.concatenate([row, row], axis=1))


def hopped(blocks, hopping):
    empty = jnp.zeros_like(hopping)
    both = jnp.concatenate(
        [
            jnp.concatenate([hopping, empty], axis=1),
            jnp.concatenate([empty, hopping], axis=1),
        ],
        axis=0,
    )
    return lax.dot_general(
        blocks, both, (((1,), (1,)), ((), ())), preferred_element_type=jnp.float32
    )


def own_gain(coupling):
    gain = gain_of(coupling, lax.axis_index("orb") * ROWS, ROWS)
    return jnp.concatenate([gain] * ROUNDS, axis=0)


LAST = pl.BlockSpec((1, 1, COLS, WIDE), lambda i: (ROUNDS - 1, TIMES // ROUNDS - 1, 0, 0))


def plain(shape):
    return pl.BlockSpec(shape, lambda i: (0,) * len(shape))


def head_kernel(last, coupling, payload):
    sigma = self_energy(last[0, 0], own_gain(coupling[...]))
    for z in range(ZS):
        payload[z] = sigma


def head(rows_of, coupling):
    shape = (ZS, COLS, WIDE)
    return pl.pallas_call(
        head_kernel,
        grid=(1,),
        in_specs=[LAST, plain((1, ORB))],
        out_specs=plain(shape),
        out_shape=jax.ShapeDtypeStruct(shape, jnp.bfloat16),
        compiler_params=pltpu.CompilerParams(vmem_limit_bytes=56 * 1024 * 1024),
        name="head",
    )(rows_of, coupling)


def ring_sum(pieces):
    a, b, c, d = pieces
    return (a + c) + (b + d)


def collect(place, riders, out):
    x, y = place[3], place[4]
    firsts, (b0, b1, low_two, high_two, b3) = riders[:XS], riders[XS:]
    source = lax.rem(x + 1, XS)

    def rider(index):
        rows = []
        for i in range(YS):
            slab = firsts[0][lax.rem(y - i + YS, YS), index]
            for d in range(1, XS):
                slab = jnp.where(source == d, firsts[d][lax.rem(y - i + YS, YS), index], slab)
            rows.append(slab)
        return jnp.concatenate(rows, axis=0)

    newest = joined(rider(0), rider(1))
    corner = stepped(rider(2), hermitian(newest)).astype(jnp.bfloat16)
    for i in range(YS):
        rings = []
        for dy in range(YS):
            if dy == 2:
                slabs = [low_two[0, i], low_two[1, i], high_two[0, i], high_two[1, i]]
            else:
                piece = (b0, b1, None, b3)[dy]
                slabs = [piece[dx, i] for dx in range(XS)]
            rings.append(ring_sum([slab.astype(jnp.float32) for slab in slabs]))
        out[COLS + i * ROWS : COLS + (i + 1) * ROWS] = ring_sum(rings)
    out[COLS + ORB :] = corner.astype(jnp.float32)


def collide_kernel(place, own, other, *refs):
    pieces, riders = refs[:9], refs[9:-4]
    mine, swapped, total, factor = refs[-4:]
    a0, a1, a2, a3, b0, b1, low_two, high_two, b3 = pieces
    step = pl.program_id(0)
    core, x, y = place[0], place[3], place[4]
    firsts = (a0, a1, a2, a3)
    sources = [lax.rem(x - dx + XS, XS) for dx in range(XS)]
    empty = jnp.zeros((ORB, WIDE), jnp.bfloat16)

    @pl.when(step == 0)
    def _():
        total[...] = jnp.zeros_like(total)
        factor[...] = jnp.zeros_like(factor)

    for dy in range(YS):
        row = pl.multiple_of(lax.rem(y - dy + YS, YS) * ROWS, ROWS)
        for dx in range(XS):
            if dy == 2:
                piece = (low_two, high_two)[dx // 2].at[dx % 2]
            else:
                piece = (b0, b1, None, b3)[dy].at[dx]
            for z in range(DEEP):
                base = (dx * DEEP + z) * WIDE
                for r in range(HALF):
                    slab = piece[z * HALF + r]
                    factor[r, pl.ds(base + row, ROWS), :WIDE] = slab
                    factor[r, pl.ds(base + ORB + row, ROWS), WIDE:] = slab

    for a in range(ROUNDS):
        low, count = a * ROWS, COLS - a * ROWS
        sides = []
        for table, target in ((own, place[1]), (other, place[2])):
            blocks = []
            for dx in range(XS):
                for z in range(DEEP):
                    block = table[a, sources[dx], z, 0, low:, :]
                    time = (sources[dx] * ZS + step * DEEP + z) * CORES + core
                    diagonal = jnp.where(
                        time <= target, block[:ROWS], jnp.zeros_like(block[:ROWS])
                    )
                    if count > ROWS:
                        diagonal = jnp.concatenate([diagonal, block[ROWS:]], axis=0)
                    blocks.append(diagonal)
            sides.append(jnp.concatenate(blocks, axis=1))
        if a < HALF:
            blocks = []
            for dx in range(XS):
                for z in range(DEEP):
                    block = jnp.concatenate(
                        [
                            firsts[dx][lax.rem(y - i + YS, YS), z * HALF + a]
                            for i in range(YS)
                        ],
                        axis=0,
                    )
                    blocks.append(jnp.concatenate([block, empty], axis=1))
                    blocks.append(jnp.concatenate([empty, block], axis=1))
            right = jnp.concatenate(blocks, axis=0)
        else:
            right = factor[a - HALF]
        product = jnp.dot(
            jnp.concatenate(sides, axis=0), right, preferred_element_type=jnp.float32
        )
        total[0, low:, :] += product[:count]
        total[1, low:, :] += product[count:]

    @pl.when(step == STEPS - 1)
    def _():
        for side, out in enumerate((mine, swapped)):
            out[:COLS] = total[side, :, :WIDE] + times_i(total[side, :, WIDE:])
        if riders:
            collect(place, riders, swapped)


def collide(place, own, other, first, second):
    half = pl.BlockSpec(
        (ROUNDS, XS, DEEP, 1, COLS, WIDE), lambda i, p: (0, 0, i, p[0], 0, 0)
    )
    pieces = first + second
    specs = [
        pl.BlockSpec((piece.shape[0], DEEP * HALF, ROWS, WIDE), lambda i, p: (0, i, 0, 0))
        for piece in pieces
    ]
    riding = first[0].shape[1] > GROUP
    riders = pieces if riding else []
    for piece in riders:
        extra = piece.shape[1] - GROUP
        specs.append(
            pl.BlockSpec(
                (piece.shape[0], extra, ROWS, WIDE),
                lambda i, p, at=GROUP // extra: (0, at, 0, 0),
            )
        )
    rows = (COLS, COLS + 2 * ORB if riding else COLS)
    return pl.pallas_call(
        collide_kernel,
        grid_spec=pltpu.PrefetchScalarGridSpec(
            num_scalar_prefetch=1,
            grid=(STEPS,),
            in_specs=[half, half] + specs,
            out_specs=[pl.BlockSpec((n, WIDE), lambda i, p: (0, 0)) for n in rows],
            scratch_shapes=[
                pltpu.VMEM((2, COLS, 2 * WIDE), jnp.float32),
                pltpu.VMEM((HALF, XS * DEEP * WIDE, 2 * WIDE), jnp.bfloat16),
            ],
        ),
        out_shape=[jax.ShapeDtypeStruct((n, WIDE), jnp.float32) for n in rows],
        compiler_params=pltpu.CompilerParams(vmem_limit_bytes=48 * 1024 * 1024),
        name="collide",
    )(place, own, other, *pieces, *riders)


def pair(value):
    high = value.astype(jnp.bfloat16)
    return high, (value - high.astype(jnp.float32)).astype(jnp.bfloat16)


def joined(high, low):
    return high.astype(jnp.float32) + low.astype(jnp.float32)


def update_kernel(ours, theirs, last, hopping, coupling, row_out, payload):
    older = last[0, 0]
    change = hopped(older, hopping[...]) + STEP * (ours[...] + theirs[...])
    row = stepped(older, change).astype(jnp.bfloat16)
    sigma = self_energy(row, own_gain(coupling[...]))
    row_out[...] = row
    overlap = lax.dot_general(
        row, sigma, (((0,), (0,)), ((), ())), preferred_element_type=jnp.float32
    )
    column = (times_i(overlap[ORB:]) - overlap[:ORB]).astype(jnp.bfloat16)
    riders = pair(change[COLS - ROWS :]) + (older[COLS - ROWS :], column)
    whole = jnp.concatenate((sigma,) + riders, axis=0)
    for z in range(ZS):
        payload[z] = whole


def update(ours, theirs, rows_of, hopping, coupling):
    shapes = [(COLS, WIDE), (ZS, COLS + EXTRA * ROWS + ORB, WIDE)]
    return pl.pallas_call(
        update_kernel,
        grid=(1,),
        in_specs=[
            plain((COLS, WIDE)),
            plain((COLS, WIDE)),
            LAST,
            plain((ORB, ORB)),
            plain((1, ORB)),
        ],
        out_specs=[plain(shape) for shape in shapes],
        out_shape=[jax.ShapeDtypeStruct(shape, jnp.bfloat16) for shape in shapes],
        compiler_params=pltpu.CompilerParams(vmem_limit_bytes=56 * 1024 * 1024),
        name="update",
    )(ours, theirs, rows_of, hopping, coupling)


def close_kernel(ours, kept, theirs, row, hopping, coupling, *refs):
    row_two, corner_one, edge_two, corner_two, lines = refs
    hop = hopping[...]
    on_last = lax.axis_index("core") == 1
    corner = jnp.where(on_last, kept[COLS + ORB :], theirs[COLS + ORB :]).astype(jnp.bfloat16)
    column = kept[COLS : COLS + ORB] + theirs[COLS : COLS + ORB]
    corner_factor = matrix_of(self_energy(corner, gain_of(coupling[...], 0, ORB)))
    older = row[...]
    change = (
        hopped(older, hop)
        + jnp.dot(older, corner_factor, preferred_element_type=jnp.float32)
        + STEP * (ours[...] + theirs[:COLS])
    )
    row_two[...] = stepped(older, change).astype(jnp.bfloat16)
    edge_change = hopped(corner, hop) + STEP * (
        column + jnp.dot(corner, corner_factor, preferred_element_type=jnp.float32)
    )
    lines[0] = corner.astype(jnp.float32)
    lines[1] = stepped(corner, edge_change)
    lines[2] = stepped(corner, hermitian(edge_change))
    own = pl.ds(pl.multiple_of(lax.axis_index("orb") * ROWS, ROWS), ROWS)
    for i, out in enumerate((corner_one, edge_two, corner_two)):
        out[...] = lines[i, own, :].astype(jnp.bfloat16)


def close(ours, kept, theirs, row, hopping, coupling):
    shapes = [(COLS, WIDE)] + [(ROWS, WIDE)] * 3
    return pl.pallas_call(
        close_kernel,
        out_shape=[jax.ShapeDtypeStruct(shape, jnp.bfloat16) for shape in shapes],
        scratch_shapes=[pltpu.VMEM((3, ORB, WIDE), jnp.float32)],
        name="close",
    )(ours, kept, theirs, row, hopping, coupling)


def body(history, hopping, coupling):
    x, z = lax.axis_index("x"), lax.axis_index("z")
    core, y = lax.axis_index("core"), lax.axis_index("orb")
    owner = (x * ZS + z) * CORES + core
    place = jnp.stack([core, owner, owner + 1 - 2 * core, x, y]).astype(jnp.int32)
    table = history.reshape(ROUNDS, XS, ZS, CORES, COLS, WIDE)
    rows_of = history.reshape(ROUNDS, TIMES // ROUNDS, COLS, WIDE)
    coupling = coupling.reshape(1, ORB)

    def along_both(first, second):
        first, second = lax.optimization_barrier((first, second))
        first, second = around(first, "orb"), around(second, "x")
        first, second = lax.optimization_barrier((first, second))
        first, second = jnp.concatenate(first), jnp.concatenate(second)
        first, second = lax.optimization_barrier((first, second))
        return along_again(first, second)

    def along_again(first, second):
        ahead = lax.ppermute(second, "orb", [(i, (i + 1) % YS) for i in range(YS)])
        behind = lax.ppermute(second, "orb", [(i, (i + 3) % YS) for i in range(YS)])
        middle = second.shape[0] // 2
        low = lax.ppermute(ahead[:middle], "orb", [(i, (i + 1) % YS) for i in range(YS)])
        high = lax.ppermute(behind[middle:], "orb", [(i, (i + 3) % YS) for i in range(YS)])
        first = [piece.reshape(YS, -1, ROWS, WIDE) for piece in around(first, "x")]
        second = [
            piece.reshape(-1, second.shape[0] // XS, ROWS, WIDE)
            for piece in (second, ahead, low, high, behind)
        ]
        return lax.optimization_barrier((first, second))

    def plane_parts(planes):
        parts = planes.reshape(ZS, -1, ROWS, WIDE)
        return (
            parts[:, :HALF].reshape(GROUP, ROWS, WIDE),
            parts[:, HALF:ROUNDS].reshape(GROUP, ROWS, WIDE),
        )

    other = swap_cores(table)
    planes = lax.all_to_all(head(rows_of, coupling), "z", 0, 0)
    planes, other = lax.optimization_barrier((planes, other))
    first, second = along_both(*plane_parts(planes))
    ours, swapped = collide(place, table, other, first, second)
    row_one, payload = update(ours, swap_cores(swapped), rows_of, hopping, coupling)

    planes = lax.all_to_all(payload, "z", 0, 0)
    first, second = plane_parts(planes)
    parts = planes.reshape(ZS, -1, ROWS, WIDE)
    riders = parts[ZS - 1, ROUNDS : ROUNDS + EXTRA]
    column = jnp.sum(parts[:, ROUNDS + EXTRA :].astype(jnp.float32), axis=0)
    first, second = along_both(
        jnp.concatenate([first, riders]),
        jnp.concatenate([second, column.astype(jnp.bfloat16)]),
    )
    ours, swapped = collide(place, table, other, first, second)
    row_two, corner_one, edge_two, corner_two = close(
        ours, swapped, swap_cores(swapped), row_one, hopping, coupling
    )
    shape = (ROUNDS, 1, ROWS, WIDE)
    return (row_one.reshape(shape), corner_one, row_two.reshape(shape), edge_two, corner_two)


def solution(mesh):
    fine = Mesh(mesh.devices.reshape(XS, ZS, CORES, YS), ("x", "z", "core", "orb"))
    tm = ("x", "z", "core")
    return jax.shard_map(
        body,
        mesh=fine,
        in_specs=(P(None, None, None, tm, "orb", None), P(), P()),
        out_specs=(
            P(None, tm, "orb", None),
            P("orb", None),
            P(None, tm, "orb", None),
            P("orb", None),
            P("orb", None),
        ),
        check_vma=False,
    )
```

```python
import jax
import jax.numpy as jnp
from jax import lax
from jax.experimental import pallas as pl
from jax.experimental.pallas import tpu as pltpu
from jax.sharding import Mesh, PartitionSpec as P

STEP = 0.08
XS, ZS, CORES, YS = 4, 8, 2, 4
ROUNDS = 6
ORB = 64
ROWS = ORB // YS
WIDE = 2 * ORB
COLS = ROUNDS * ROWS
TIMES = ROUNDS * XS * ZS * CORES
EXTRA = 3
HALF = ROUNDS // 2
GROUP = ZS * HALF
SMALL = pltpu.CompilerParams(vmem_limit_bytes=8 * 1024 * 1024)


def swap_cores(array):
    return lax.ppermute(array, "core", [(0, 1), (1, 0)])


def around(array, axis):
    pieces = {0: array}
    for distance in (1, 3, 2):
        pairs = [(i, (i + distance) % 4) for i in range(4)]
        pieces[distance] = lax.ppermute(array, axis, pairs)
    return [pieces[d] for d in range(4)]


def halves_swapped(value):
    return jnp.concatenate([value[:, ORB:], value[:, :ORB]], axis=-1)


def times_i(value):
    return jnp.concatenate([-value[:, ORB:], value[:, :ORB]], axis=-1)


def matrix_of(value):
    return jnp.concatenate([value, times_i(value)], axis=0)


def stepped(older, change):
    return older.astype(jnp.float32) - STEP * times_i(change)


def self_energy(blocks, gain):
    parts = blocks.astype(jnp.float32)
    square = parts * parts
    return (gain * (square + halves_swapped(square)) * parts).astype(jnp.bfloat16)


def hermitian(whole):
    real_part = whole[:, :ORB]
    imag_part = whole[:, ORB:]
    return jnp.concatenate([real_part + real_part.T, imag_part - imag_part.T], axis=-1)


def gain_of(row, first, count):
    lane = lax.broadcasted_iota(jnp.int32, (count, ORB), 1)
    line = lax.broadcasted_iota(jnp.int32, (count, ORB), 0)
    mine = jnp.where(lane == line + first, jnp.broadcast_to(row, (count, ORB)), 0.0)
    column = jnp.sum(mine, axis=1, keepdims=True)
    return -(column * jnp.concatenate([row, row], axis=1))


def hopped(blocks, hopping):
    empty = jnp.zeros_like(hopping)
    both = jnp.concatenate(
        [
            jnp.concatenate([hopping, empty], axis=1),
            jnp.concatenate([empty, hopping], axis=1),
        ],
        axis=0,
    )
    return lax.dot_general(
        blocks, both, (((1,), (1,)), ((), ())), preferred_element_type=jnp.float32
    )


def own_gain(coupling):
    gain = gain_of(coupling, lax.axis_index("orb") * ROWS, ROWS)
    return jnp.concatenate([gain] * ROUNDS, axis=0)


LAST = pl.BlockSpec((1, 1, COLS, WIDE), lambda i: (ROUNDS - 1, TIMES // ROUNDS - 1, 0, 0))


def plain(shape):
    return pl.BlockSpec(shape, lambda i: (0,) * len(shape))


def head_kernel(last, coupling, payload, row):
    row[...] = last[0, 0]
    sigma = self_energy(last[0, 0], own_gain(coupling[...]))
    for z in range(ZS):
        payload[z] = sigma


def head(rows_of, coupling):
    shape = (ZS, COLS, WIDE)
    return pl.pallas_call(
        head_kernel,
        grid=(1,),
        in_specs=[LAST, plain((1, ORB))],
        out_specs=[plain(shape), plain((COLS, WIDE))],
        out_shape=[
            jax.ShapeDtypeStruct(shape, jnp.bfloat16),
            jax.ShapeDtypeStruct((COLS, WIDE), jnp.bfloat16),
        ],
        compiler_params=pltpu.CompilerParams(vmem_limit_bytes=56 * 1024 * 1024),
        name="head",
    )(rows_of, coupling)


def ring_sum(pieces):
    a, b, c, d = pieces
    return (a + c) + (b + d)


def collect(place, riders, out):
    x, y = place[3], place[4]
    firsts, (b0, b1, low_two, high_two, b3) = riders[:XS], riders[XS:]
    source = lax.rem(x + 1, XS)

    def rider(index):
        rows = []
        for i in range(YS):
            slab = firsts[0][lax.rem(y - i + YS, YS), GROUP + index]
            for d in range(1, XS):
                other = firsts[d][lax.rem(y - i + YS, YS), GROUP + index]
                slab = jnp.where(source == d, other, slab)
            rows.append(slab)
        return jnp.concatenate(rows, axis=0)

    newest = joined(rider(0), rider(1))
    corner = stepped(rider(2), hermitian(newest)).astype(jnp.bfloat16)
    for i in range(YS):
        rings = []
        for dy in range(YS):
            if dy == 2:
                halves = (low_two, high_two)
                slabs = [halves[dx // 2][dx % 2, GROUP + i] for dx in range(XS)]
            else:
                piece = (b0, b1, None, b3)[dy]
                slabs = [piece[dx, GROUP + i] for dx in range(XS)]
            rings.append(ring_sum([slab.astype(jnp.float32) for slab in slabs]))
        out[2 * COLS + i * ROWS : 2 * COLS + (i + 1) * ROWS] = ring_sum(rings)
    out[2 * COLS + ORB :] = corner.astype(jnp.float32)


def load_kernel(core, own, other, *refs):
    buffers, arrived = refs[:-1], refs[-1]
    copies = []
    for a in range(ROUNDS):
        rows = pl.ds(a * ROWS, COLS - a * ROWS)
        for side, table in enumerate((own, other)):
            i = a * CORES + side
            copies.append(
                pltpu.make_async_copy(
                    table.at[a, :, :, core[0], rows, :], buffers[i], arrived.at[i]
                )
            )
            copies[-1].start()
    for copy in copies:
        copy.wait()


def load(core, own, other):
    far = pl.BlockSpec(memory_space=pl.ANY)
    counts = [COLS - a * ROWS for a in range(ROUNDS) for _ in range(CORES)]
    return pl.pallas_call(
        load_kernel,
        in_specs=[pl.BlockSpec(memory_space=pltpu.SMEM), far, far],
        out_specs=[pl.BlockSpec(memory_space=pltpu.VMEM)] * len(counts),
        out_shape=[
            jax.ShapeDtypeStruct((XS, ZS, count, WIDE), jnp.bfloat16) for count in counts
        ],
        scratch_shapes=[pltpu.SemaphoreType.DMA((len(counts),))],
        compiler_params=pltpu.CompilerParams(vmem_limit_bytes=16 * 1024 * 1024),
        cost_estimate=pl.CostEstimate(
            flops=0, bytes_accessed=12000000, transcendentals=0
        ),
        name="load",
    )(core, own, other)


PARTS = 1


def collide_kernel(place, *refs):
    buffers, refs = refs[: ROUNDS * CORES], refs[ROUNDS * CORES :]
    pieces, out, total, factor = refs[:9], refs[9], refs[10], refs[11]
    a0, a1, a2, a3, b0, b1, low_two, high_two, b3 = pieces
    core, x, y = place[0], place[3], place[4]
    firsts = (a0, a1, a2, a3)
    sources = [lax.rem(x - dx + XS, XS) for dx in range(XS)]
    empty = jnp.zeros((ORB, WIDE), jnp.bfloat16)
    for dy in range(YS):
        row = pl.multiple_of(lax.rem(y - dy + YS, YS) * ROWS, ROWS)
        for dx in range(XS):
            if dy == 2:
                piece = (low_two, high_two)[dx // 2].at[dx % 2]
            else:
                piece = (b0, b1, None, b3)[dy].at[dx]
            for z in range(ZS):
                for r in range(HALF):
                    factor[r, dx * ZS + z, pl.ds(row, ROWS), :] = piece[z * HALF + r]

    for a in range(ROUNDS):
        low, count = a * ROWS, COLS - a * ROWS
        for part in range(PARTS):
            groups = [
                (dx, z)
                for dx in range(part * XS // PARTS, (part + 1) * XS // PARTS)
                for z in range(ZS)
            ]
            sides = []
            for side, target in enumerate((place[1], place[2])):
                table = buffers[a * CORES + side]
                blocks = []
                for dx, z in groups:
                    block = table[sources[dx], z]
                    time = (sources[dx] * ZS + z) * CORES + core
                    diagonal = jnp.where(
                        time <= target, block[:ROWS], jnp.zeros_like(block[:ROWS])
                    )
                    if count > ROWS:
                        diagonal = jnp.concatenate([diagonal, block[ROWS:]], axis=0)
                    blocks.append(diagonal)
                sides.append(jnp.concatenate(blocks, axis=1))
            blocks = []
            for dx, z in groups:
                if a < HALF:
                    block = jnp.concatenate(
                        [
                            firsts[dx][lax.rem(y - i + YS, YS), z * HALF + a]
                            for i in range(YS)
                        ],
                        axis=0,
                    )
                else:
                    block = factor[a - HALF, dx * ZS + z]
                blocks.append(jnp.concatenate([block, empty], axis=1))
                blocks.append(jnp.concatenate([empty, block], axis=1))
            product = jnp.dot(
                jnp.concatenate(sides, axis=0),
                jnp.concatenate(blocks, axis=0),
                preferred_element_type=jnp.float32,
            )
            if a == 0 and part == 0:
                total[0], total[1] = product[:count], product[count:]
            else:
                total[0, low:, :] += product[:count]
                total[1, low:, :] += product[count:]

    for side in range(2):
        rows = pl.ds(side * COLS, COLS)
        out[rows, :] = total[side, :, :WIDE] + times_i(total[side, :, WIDE:])
    if pieces[0].shape[1] > GROUP:
        collect(place, pieces, out)


def collide(place, history, first, second):
    pieces = first + second
    riding = first[0].shape[1] > GROUP
    shape = (2 * COLS + (2 * ORB if riding else 0), WIDE)
    whole = pl.BlockSpec(memory_space=pltpu.VMEM)
    return pl.pallas_call(
        collide_kernel,
        in_specs=[pl.BlockSpec(memory_space=pltpu.SMEM)]
        + [whole] * (len(history) + len(pieces)),
        out_specs=whole,
        scratch_shapes=[
            pltpu.VMEM((2, COLS, 2 * WIDE), jnp.float32),
            pltpu.VMEM((HALF, XS * ZS, ORB, WIDE), jnp.bfloat16),
        ],
        out_shape=jax.ShapeDtypeStruct(shape, jnp.float32),
        compiler_params=pltpu.CompilerParams(vmem_limit_bytes=24 * 1024 * 1024),
        name="collide",
    )(place, *history, *pieces)


def pair(value):
    high = value.astype(jnp.bfloat16)
    return high, (value - high.astype(jnp.float32)).astype(jnp.bfloat16)


def joined(high, low):
    return high.astype(jnp.float32) + low.astype(jnp.float32)


def update_kernel(sums, theirs, last, hopping, coupling, row_out, payload):
    older = last[...]
    change = hopped(older, hopping[...]) + STEP * (sums[:COLS] + theirs[...])
    row = stepped(older, change).astype(jnp.bfloat16)
    sigma = self_energy(row, own_gain(coupling[...]))
    row_out[...] = row
    overlap = lax.dot_general(
        row, sigma, (((0,), (0,)), ((), ())), preferred_element_type=jnp.float32
    )
    column = (times_i(overlap[ORB:]) - overlap[:ORB]).astype(jnp.bfloat16)
    riders = pair(change[COLS - ROWS :]) + (older[COLS - ROWS :], column)
    whole = jnp.concatenate((sigma,) + riders, axis=0)
    for z in range(ZS):
        payload[z] = whole


def update(sums, theirs, last, hopping, coupling):
    shapes = [(COLS, WIDE), (ZS, COLS + EXTRA * ROWS + ORB, WIDE)]
    return pl.pallas_call(
        update_kernel,
        out_shape=[jax.ShapeDtypeStruct(shape, jnp.bfloat16) for shape in shapes],
        compiler_params=SMALL,
        name="update",
    )(sums, theirs, last, hopping, coupling)


def close_kernel(sums, theirs, row, hopping, coupling, *refs):
    row_two, corner_one, edge_two, corner_two, lines = refs
    hop = hopping[...]
    on_last = lax.axis_index("core") == 1
    corner = jnp.where(on_last, sums[2 * COLS + ORB :], theirs[COLS + ORB :]).astype(jnp.bfloat16)
    column = sums[2 * COLS : 2 * COLS + ORB] + theirs[COLS : COLS + ORB]
    corner_factor = matrix_of(self_energy(corner, gain_of(coupling[...], 0, ORB)))
    older = row[...]
    change = (
        hopped(older, hop)
        + jnp.dot(older, corner_factor, preferred_element_type=jnp.float32)
        + STEP * (sums[:COLS] + theirs[:COLS])
    )
    row_two[...] = stepped(older, change).astype(jnp.bfloat16)
    edge_change = hopped(corner, hop) + STEP * (
        column + jnp.dot(corner, corner_factor, preferred_element_type=jnp.float32)
    )
    lines[0] = corner.astype(jnp.float32)
    lines[1] = stepped(corner, edge_change)
    lines[2] = stepped(corner, hermitian(edge_change))
    own = pl.ds(pl.multiple_of(lax.axis_index("orb") * ROWS, ROWS), ROWS)
    for i, out in enumerate((corner_one, edge_two, corner_two)):
        out[...] = lines[i, own, :].astype(jnp.bfloat16)


def close(sums, theirs, row, hopping, coupling):
    shapes = [(COLS, WIDE)] + [(ROWS, WIDE)] * 3
    return pl.pallas_call(
        close_kernel,
        out_shape=[jax.ShapeDtypeStruct(shape, jnp.bfloat16) for shape in shapes],
        scratch_shapes=[pltpu.VMEM((3, ORB, WIDE), jnp.float32)],
        compiler_params=SMALL,
        name="close",
    )(sums, theirs, row, hopping, coupling)


def body(history, hopping, coupling):
    x, z = lax.axis_index("x"), lax.axis_index("z")
    core, y = lax.axis_index("core"), lax.axis_index("orb")
    owner = (x * ZS + z) * CORES + core
    place = jnp.stack([core, owner, owner + 1 - 2 * core, x, y]).astype(jnp.int32)
    table = history.reshape(ROUNDS, XS, ZS, CORES, COLS, WIDE)
    rows_of = history.reshape(ROUNDS, TIMES // ROUNDS, COLS, WIDE)
    coupling = coupling.reshape(1, ORB)

    def along_one(first, second):
        first, second = lax.optimization_barrier((first, second))
        first, second = around(first, "orb"), around(second, "x")
        first, second = lax.optimization_barrier((first, second))
        first, second = jnp.concatenate(first), jnp.concatenate(second)
        return lax.optimization_barrier((first, second))

    def along_again(first, second):
        ahead = lax.ppermute(second, "orb", [(i, (i + 1) % YS) for i in range(YS)])
        behind = lax.ppermute(second, "orb", [(i, (i + 3) % YS) for i in range(YS)])
        middle = second.shape[0] // 2
        low = lax.ppermute(ahead[:middle], "orb", [(i, (i + 1) % YS) for i in range(YS)])
        high = lax.ppermute(behind[middle:], "orb", [(i, (i + 3) % YS) for i in range(YS)])
        first = [piece.reshape(YS, -1, ROWS, WIDE) for piece in around(first, "x")]
        second = [
            piece.reshape(-1, second.shape[0] // XS, ROWS, WIDE)
            for piece in (second, ahead, low, high, behind)
        ]
        return lax.optimization_barrier((first, second))

    def plane_parts(planes):
        parts = planes.reshape(ZS, -1, ROWS, WIDE)
        return (
            parts[:, :HALF].reshape(GROUP, ROWS, WIDE),
            parts[:, HALF:ROUNDS].reshape(GROUP, ROWS, WIDE),
        )

    other = swap_cores(table)
    payload, last_row = head(rows_of, coupling)
    planes = lax.all_to_all(payload, "z", 0, 0)
    planes, other = lax.optimization_barrier((planes, other))
    first, second = along_one(*plane_parts(planes))
    first, second, own, other, place = lax.optimization_barrier(
        (first, second, table, other, place)
    )
    history = load(place[:1], own, other)
    first, second = along_again(first, second)
    sums = collide(place, history, first, second)
    row_one, payload = update(sums, swap_cores(sums[COLS:]), last_row, hopping, coupling)

    planes = lax.all_to_all(payload, "z", 0, 0)
    first, second = plane_parts(planes)
    parts = planes.reshape(ZS, -1, ROWS, WIDE)
    riders = parts[ZS - 1, ROUNDS : ROUNDS + EXTRA]
    column = jnp.sum(parts[:, ROUNDS + EXTRA :].astype(jnp.float32), axis=0)
    first, second = along_again(
        *along_one(
            jnp.concatenate([first, riders]),
            jnp.concatenate([second, column.astype(jnp.bfloat16)]),
        )
    )
    sums = collide(place, history, first, second)
    row_two, corner_one, edge_two, corner_two = close(
        sums, swap_cores(sums[COLS:]), row_one, hopping, coupling
    )
    shape = (ROUNDS, 1, ROWS, WIDE)
    return (row_one.reshape(shape), corner_one, row_two.reshape(shape), edge_two, corner_two)


def solution(mesh):
    fine = Mesh(mesh.devices.reshape(XS, ZS, CORES, YS), ("x", "z", "core", "orb"))
    tm = ("x", "z", "core")
    return jax.shard_map(
        body,
        mesh=fine,
        in_specs=(P(None, None, None, tm, "orb", None), P(), P()),
        out_specs=(
            P(None, tm, "orb", None),
            P("orb", None),
            P(None, tm, "orb", None),
            P("orb", None),
            P("orb", None),
        ),
        check_vma=False,
    )
```

```python
import jax
import jax.numpy as jnp
from jax import lax
from jax.experimental import pallas as pl
from jax.experimental.pallas import tpu as pltpu
from jax.sharding import Mesh, PartitionSpec as P

STEP = 0.08
XS, ZS, CORES, YS = 4, 8, 2, 4
ROUNDS = 6
ORB = 64
ROWS = ORB // YS
WIDE = 2 * ORB
COLS = ROUNDS * ROWS
TIMES = ROUNDS * XS * ZS * CORES
EXTRA = 3
HALF = ROUNDS // 2
GROUP = ZS * HALF
SMALL = pltpu.CompilerParams(vmem_limit_bytes=8 * 1024 * 1024)


def swap_cores(array):
    return lax.ppermute(array, "core", [(0, 1), (1, 0)])


def around(array, axis):
    pieces = {0: array}
    for distance in (1, 3, 2):
        pairs = [(i, (i + distance) % 4) for i in range(4)]
        pieces[distance] = lax.ppermute(array, axis, pairs)
    return [pieces[d] for d in range(4)]


def halves_swapped(value):
    return jnp.concatenate([value[:, ORB:], value[:, :ORB]], axis=-1)


def times_i(value):
    return jnp.concatenate([-value[:, ORB:], value[:, :ORB]], axis=-1)


def matrix_of(value):
    return jnp.concatenate([value, times_i(value)], axis=0)


def stepped(older, change):
    return older.astype(jnp.float32) - STEP * times_i(change)


def self_energy(blocks, gain):
    parts = blocks.astype(jnp.float32)
    square = parts * parts
    return (gain * (square + halves_swapped(square)) * parts).astype(jnp.bfloat16)


def hermitian(whole):
    real_part = whole[:, :ORB]
    imag_part = whole[:, ORB:]
    return jnp.concatenate([real_part + real_part.T, imag_part - imag_part.T], axis=-1)


def gain_of(row, first, count):
    lane = lax.broadcasted_iota(jnp.int32, (count, ORB), 1)
    line = lax.broadcasted_iota(jnp.int32, (count, ORB), 0)
    mine = jnp.where(lane == line + first, jnp.broadcast_to(row, (count, ORB)), 0.0)
    column = jnp.sum(mine, axis=1, keepdims=True)
    return -(column * jnp.concatenate([row, row], axis=1))


def hopped(blocks, hopping):
    empty = jnp.zeros_like(hopping)
    both = jnp.concatenate(
        [
            jnp.concatenate([hopping, empty], axis=1),
            jnp.concatenate([empty, hopping], axis=1),
        ],
        axis=0,
    )
    return lax.dot_general(
        blocks, both, (((1,), (1,)), ((), ())), preferred_element_type=jnp.float32
    )


def own_gain(coupling):
    gain = gain_of(coupling, lax.axis_index("orb") * ROWS, ROWS)
    return jnp.concatenate([gain] * ROUNDS, axis=0)


LAST = pl.BlockSpec((1, 1, COLS, WIDE), lambda i: (ROUNDS - 1, TIMES // ROUNDS - 1, 0, 0))


def plain(shape):
    return pl.BlockSpec(shape, lambda i: (0,) * len(shape))


def head_kernel(last, coupling, payload, row):
    row[...] = last[0, 0]
    sigma = self_energy(last[0, 0], own_gain(coupling[...]))
    for z in range(ZS):
        payload[z] = sigma


def head(rows_of, coupling):
    shape = (ZS, COLS, WIDE)
    return pl.pallas_call(
        head_kernel,
        grid=(1,),
        in_specs=[LAST, plain((1, ORB))],
        out_specs=[plain(shape), plain((COLS, WIDE))],
        out_shape=[
            jax.ShapeDtypeStruct(shape, jnp.bfloat16),
            jax.ShapeDtypeStruct((COLS, WIDE), jnp.bfloat16),
        ],
        compiler_params=pltpu.CompilerParams(vmem_limit_bytes=56 * 1024 * 1024),
        name="head",
    )(rows_of, coupling)


def ring_sum(pieces):
    a, b, c, d = pieces
    return (a + c) + (b + d)


def piece_at(pieces, distance, index, slot):
    if distance != 2:
        return pieces[(0, 1, None, 4)[distance]][index, slot]
    near = lax.rem(index, 2)
    return jnp.where(index < 2, pieces[2][near, slot], pieces[3][near, slot])


def collect(place, riders, out):
    x, y = place[3], place[4]
    firsts, (b0, b1, low_two, high_two, b3) = riders[:5], riders[5:]
    source = lax.rem(x + 1, XS)

    def rider(index):
        rows = []
        for i in range(YS):
            at = lax.rem(y - i + YS, YS)
            slab = piece_at(firsts, 0, at, GROUP + index)
            for d in range(1, XS):
                other = piece_at(firsts, d, at, GROUP + index)
                slab = jnp.where(source == d, other, slab)
            rows.append(slab)
        return jnp.concatenate(rows, axis=0)

    newest = joined(rider(0), rider(1))
    corner = stepped(rider(2), hermitian(newest)).astype(jnp.bfloat16)
    for i in range(YS):
        rings = []
        for dy in range(YS):
            if dy == 2:
                halves = (low_two, high_two)
                slabs = [halves[dx // 2][dx % 2, GROUP + i] for dx in range(XS)]
            else:
                piece = (b0, b1, None, b3)[dy]
                slabs = [piece[dx, GROUP + i] for dx in range(XS)]
            rings.append(ring_sum([slab.astype(jnp.float32) for slab in slabs]))
        out[2 * COLS + i * ROWS : 2 * COLS + (i + 1) * ROWS] = ring_sum(rings)
    out[2 * COLS + ORB :] = corner.astype(jnp.float32)


def load_kernel(core, own, other, *refs):
    buffers, arrived = refs[:-1], refs[-1]
    copies = []
    for a in range(ROUNDS):
        rows = pl.ds(a * ROWS, COLS - a * ROWS)
        for side, table in enumerate((own, other)):
            i = a * CORES + side
            copies.append(
                pltpu.make_async_copy(
                    table.at[a, :, :, core[0], rows, :], buffers[i], arrived.at[i]
                )
            )
            copies[-1].start()
    for copy in copies:
        copy.wait()


def load(core, own, other):
    far = pl.BlockSpec(memory_space=pl.ANY)
    counts = [COLS - a * ROWS for a in range(ROUNDS) for _ in range(CORES)]
    return pl.pallas_call(
        load_kernel,
        in_specs=[pl.BlockSpec(memory_space=pltpu.SMEM), far, far],
        out_specs=[pl.BlockSpec(memory_space=pltpu.VMEM)] * len(counts),
        out_shape=[
            jax.ShapeDtypeStruct((XS, ZS, count, WIDE), jnp.bfloat16) for count in counts
        ],
        scratch_shapes=[pltpu.SemaphoreType.DMA((len(counts),))],
        compiler_params=pltpu.CompilerParams(vmem_limit_bytes=47 * 1024 * 1024),
        cost_estimate=pl.CostEstimate(
            flops=0, bytes_accessed=12000000, transcendentals=0
        ),
        name="load",
    )(core, own, other)


PARTS = 1


def collide_kernel(place, *refs):
    buffers, refs = refs[: ROUNDS * CORES], refs[ROUNDS * CORES :]
    pieces, (out, total, factor) = refs[:10], refs[10:]
    firsts, (b0, b1, low_two, high_two, b3) = pieces[:5], pieces[5:]
    core, x, y = place[0], place[3], place[4]
    sources = [lax.rem(x - dx + XS, XS) for dx in range(XS)]
    empty = jnp.zeros((ORB, WIDE), jnp.bfloat16)
    for dy in range(YS):
        row = pl.multiple_of(lax.rem(y - dy + YS, YS) * ROWS, ROWS)
        for dx in range(XS):
            if dy == 2:
                piece = (low_two, high_two)[dx // 2].at[dx % 2]
            else:
                piece = (b0, b1, None, b3)[dy].at[dx]
            for z in range(ZS):
                for r in range(HALF):
                    factor[r, dx * ZS + z, pl.ds(row, ROWS), :] = piece[z * HALF + r]

    for a in range(ROUNDS):
        low, count = a * ROWS, COLS - a * ROWS
        for part in range(PARTS):
            groups = [
                (dx, z)
                for dx in range(part * XS // PARTS, (part + 1) * XS // PARTS)
                for z in range(ZS)
            ]
            sides = []
            for side, target in enumerate((place[1], place[2])):
                table = buffers[a * CORES + side]
                blocks = []
                for dx, z in groups:
                    block = table[sources[dx], z]
                    time = (sources[dx] * ZS + z) * CORES + core
                    diagonal = jnp.where(
                        time <= target, block[:ROWS], jnp.zeros_like(block[:ROWS])
                    )
                    if count > ROWS:
                        diagonal = jnp.concatenate([diagonal, block[ROWS:]], axis=0)
                    blocks.append(diagonal)
                sides.append(jnp.concatenate(blocks, axis=1))
            blocks = []
            for dx, z in groups:
                if a < HALF:
                    block = jnp.concatenate(
                        [
                            piece_at(firsts, dx, lax.rem(y - i + YS, YS), z * HALF + a)
                            for i in range(YS)
                        ],
                        axis=0,
                    )
                else:
                    block = factor[a - HALF, dx * ZS + z]
                blocks.append(jnp.concatenate([block, empty], axis=1))
                blocks.append(jnp.concatenate([empty, block], axis=1))
            product = jnp.dot(
                jnp.concatenate(sides, axis=0),
                jnp.concatenate(blocks, axis=0),
                preferred_element_type=jnp.float32,
            )
            if a == 0 and part == 0:
                total[0], total[1] = product[:count], product[count:]
            else:
                total[0, low:, :] += product[:count]
                total[1, low:, :] += product[count:]

    for side in range(2):
        rows = pl.ds(side * COLS, COLS)
        out[rows, :] = total[side, :, :WIDE] + times_i(total[side, :, WIDE:])
    if pieces[0].shape[1] > GROUP:
        collect(place, pieces, out)


def collide(place, history, first, second):
    pieces = first + second
    riding = first[0].shape[1] > GROUP
    shape = (2 * COLS + (2 * ORB if riding else 0), WIDE)
    whole = pl.BlockSpec(memory_space=pltpu.VMEM)
    return pl.pallas_call(
        collide_kernel,
        in_specs=[pl.BlockSpec(memory_space=pltpu.SMEM)]
        + [whole] * (len(history) + len(pieces)),
        out_specs=whole,
        scratch_shapes=[
            pltpu.VMEM((2, COLS, 2 * WIDE), jnp.float32),
            pltpu.VMEM((HALF, XS * ZS, ORB, WIDE), jnp.bfloat16),
        ],
        out_shape=jax.ShapeDtypeStruct(shape, jnp.float32),
        compiler_params=pltpu.CompilerParams(vmem_limit_bytes=24 * 1024 * 1024),
        name="collide",
    )(place, *history, *pieces)


def pair(value):
    high = value.astype(jnp.bfloat16)
    return high, (value - high.astype(jnp.float32)).astype(jnp.bfloat16)


def joined(high, low):
    return high.astype(jnp.float32) + low.astype(jnp.float32)


def update_kernel(sums, theirs, last, hopping, coupling, row_out, payload):
    older = last[...]
    change = hopped(older, hopping[...]) + STEP * (sums[:COLS] + theirs[...])
    row = stepped(older, change).astype(jnp.bfloat16)
    sigma = self_energy(row, own_gain(coupling[...]))
    row_out[...] = row
    overlap = lax.dot_general(
        row, sigma, (((0,), (0,)), ((), ())), preferred_element_type=jnp.float32
    )
    column = (times_i(overlap[ORB:]) - overlap[:ORB]).astype(jnp.bfloat16)
    riders = pair(change[COLS - ROWS :]) + (older[COLS - ROWS :], column)
    whole = jnp.concatenate((sigma,) + riders, axis=0)
    for z in range(ZS):
        payload[z] = whole


def update(sums, theirs, last, hopping, coupling):
    shapes = [(COLS, WIDE), (ZS, COLS + EXTRA * ROWS + ORB, WIDE)]
    return pl.pallas_call(
        update_kernel,
        out_shape=[jax.ShapeDtypeStruct(shape, jnp.bfloat16) for shape in shapes],
        compiler_params=SMALL,
        name="update",
    )(sums, theirs, last, hopping, coupling)


def close_kernel(sums, theirs, row, hopping, coupling, *refs):
    row_two, corner_one, edge_two, corner_two, lines = refs
    hop = hopping[...]
    on_last = lax.axis_index("core") == 1
    corner = jnp.where(on_last, sums[2 * COLS + ORB :], theirs[COLS + ORB :]).astype(jnp.bfloat16)
    column = sums[2 * COLS : 2 * COLS + ORB] + theirs[COLS : COLS + ORB]
    corner_factor = matrix_of(self_energy(corner, gain_of(coupling[...], 0, ORB)))
    older = row[...]
    change = (
        hopped(older, hop)
        + jnp.dot(older, corner_factor, preferred_element_type=jnp.float32)
        + STEP * (sums[:COLS] + theirs[:COLS])
    )
    row_two[...] = stepped(older, change).astype(jnp.bfloat16)
    edge_change = hopped(corner, hop) + STEP * (
        column + jnp.dot(corner, corner_factor, preferred_element_type=jnp.float32)
    )
    lines[0] = corner.astype(jnp.float32)
    lines[1] = stepped(corner, edge_change)
    lines[2] = stepped(corner, hermitian(edge_change))
    own = pl.ds(pl.multiple_of(lax.axis_index("orb") * ROWS, ROWS), ROWS)
    for i, out in enumerate((corner_one, edge_two, corner_two)):
        out[...] = lines[i, own, :].astype(jnp.bfloat16)


def close(sums, theirs, row, hopping, coupling):
    shapes = [(COLS, WIDE)] + [(ROWS, WIDE)] * 3
    return pl.pallas_call(
        close_kernel,
        out_shape=[jax.ShapeDtypeStruct(shape, jnp.bfloat16) for shape in shapes],
        scratch_shapes=[pltpu.VMEM((3, ORB, WIDE), jnp.float32)],
        compiler_params=SMALL,
        name="close",
    )(sums, theirs, row, hopping, coupling)


def body(history, hopping, coupling):
    x, z = lax.axis_index("x"), lax.axis_index("z")
    core, y = lax.axis_index("core"), lax.axis_index("orb")
    owner = (x * ZS + z) * CORES + core
    place = jnp.stack([core, owner, owner + 1 - 2 * core, x, y]).astype(jnp.int32)
    table = history.reshape(ROUNDS, XS, ZS, CORES, COLS, WIDE)
    rows_of = history.reshape(ROUNDS, TIMES // ROUNDS, COLS, WIDE)
    coupling = coupling.reshape(1, ORB)

    def along_one(first, second):
        first, second = lax.optimization_barrier((first, second))
        first, second = around(first, "orb"), around(second, "x")
        first, second = lax.optimization_barrier((first, second))
        first, second = jnp.concatenate(first), jnp.concatenate(second)
        return lax.optimization_barrier((first, second))

    def ring(array, axis):
        forward = [(i, (i + 1) % 4) for i in range(4)]
        backward = [(i, (i + 3) % 4) for i in range(4)]
        ahead = lax.ppermute(array, axis, forward)
        behind = lax.ppermute(array, axis, backward)
        middle = array.shape[0] // 2
        low = lax.ppermute(ahead[:middle], axis, forward)
        high = lax.ppermute(behind[middle:], axis, backward)
        return [
            piece.reshape(-1, array.shape[0] // 4, ROWS, WIDE)
            for piece in (array, ahead, low, high, behind)
        ]

    def along_again(first, second):
        return lax.optimization_barrier((ring(first, "x"), ring(second, "orb")))

    def plane_parts(planes):
        parts = planes.reshape(ZS, -1, ROWS, WIDE)
        return (
            parts[:, :HALF].reshape(GROUP, ROWS, WIDE),
            parts[:, HALF:ROUNDS].reshape(GROUP, ROWS, WIDE),
        )

    other = swap_cores(table)
    payload, last_row = head(rows_of, coupling)
    planes = lax.all_to_all(payload, "z", 0, 0)
    planes, other = lax.optimization_barrier((planes, other))
    first, second = along_one(*plane_parts(planes))
    first, second, own, other, place = lax.optimization_barrier(
        (first, second, table, other, place)
    )
    history = load(place[:1], own, other)
    first, second = along_again(first, second)
    sums = collide(place, history, first, second)
    row_one, payload = update(sums, swap_cores(sums[COLS:]), last_row, hopping, coupling)

    planes = lax.all_to_all(payload, "z", 0, 0)
    first, second = plane_parts(planes)
    parts = planes.reshape(ZS, -1, ROWS, WIDE)
    riders = parts[ZS - 1, ROUNDS : ROUNDS + EXTRA]
    column = jnp.sum(parts[:, ROUNDS + EXTRA :].astype(jnp.float32), axis=0)
    first, second = along_again(
        *along_one(
            jnp.concatenate([first, riders]),
            jnp.concatenate([second, column.astype(jnp.bfloat16)]),
        )
    )
    sums = collide(place, history, first, second)
    row_two, corner_one, edge_two, corner_two = close(
        sums, swap_cores(sums[COLS:]), row_one, hopping, coupling
    )
    shape = (ROUNDS, 1, ROWS, WIDE)
    return (row_one.reshape(shape), corner_one, row_two.reshape(shape), edge_two, corner_two)


def solution(mesh):
    fine = Mesh(mesh.devices.reshape(XS, ZS, CORES, YS), ("x", "z", "core", "orb"))
    tm = ("x", "z", "core")
    return jax.shard_map(
        body,
        mesh=fine,
        in_specs=(P(None, None, None, tm, "orb", None), P(), P()),
        out_specs=(
            P(None, tm, "orb", None),
            P("orb", None),
            P(None, tm, "orb", None),
            P("orb", None),
            P("orb", None),
        ),
        check_vma=False,
    )
```

```python
import jax
import jax.numpy as jnp
from jax import lax
from jax.experimental import pallas as pl
from jax.experimental.pallas import tpu as pltpu
from jax.sharding import Mesh, PartitionSpec as P

STEP = 0.08
XS, ZS, CORES, YS = 4, 8, 2, 4
ROUNDS = 6
ORB = 64
ROWS = ORB // YS
WIDE = 2 * ORB
COLS = ROUNDS * ROWS
TIMES = ROUNDS * XS * ZS * CORES
EXTRA = 3
HALF = ROUNDS // 2
GROUP = ZS * HALF
SMALL = pltpu.CompilerParams(vmem_limit_bytes=8 * 1024 * 1024)


def swap_cores(array):
    return lax.ppermute(array, "core", [(0, 1), (1, 0)])


def around(array, axis):
    pieces = {0: array}
    for distance in (1, 3, 2):
        pairs = [(i, (i + distance) % 4) for i in range(4)]
        pieces[distance] = lax.ppermute(array, axis, pairs)
    return [pieces[d] for d in range(4)]


def halves_swapped(value):
    return jnp.concatenate([value[:, ORB:], value[:, :ORB]], axis=-1)


def times_i(value):
    return jnp.concatenate([-value[:, ORB:], value[:, :ORB]], axis=-1)


def matrix_of(value):
    return jnp.concatenate([value, times_i(value)], axis=0)


def stepped(older, change):
    return older.astype(jnp.float32) - STEP * times_i(change)


def self_energy(blocks, gain):
    parts = blocks.astype(jnp.float32)
    square = parts * parts
    return (gain * (square + halves_swapped(square)) * parts).astype(jnp.bfloat16)


def hermitian(whole):
    real_part = whole[:, :ORB]
    imag_part = whole[:, ORB:]
    return jnp.concatenate([real_part + real_part.T, imag_part - imag_part.T], axis=-1)


def gain_of(row, first, count):
    lane = lax.broadcasted_iota(jnp.int32, (count, ORB), 1)
    line = lax.broadcasted_iota(jnp.int32, (count, ORB), 0)
    mine = jnp.where(lane == line + first, jnp.broadcast_to(row, (count, ORB)), 0.0)
    column = jnp.sum(mine, axis=1, keepdims=True)
    return -(column * jnp.concatenate([row, row], axis=1))


def hopped(blocks, hopping):
    empty = jnp.zeros_like(hopping)
    both = jnp.concatenate(
        [
            jnp.concatenate([hopping, empty], axis=1),
            jnp.concatenate([empty, hopping], axis=1),
        ],
        axis=0,
    )
    return lax.dot_general(
        blocks, both, (((1,), (1,)), ((), ())), preferred_element_type=jnp.float32
    )


def own_gain(coupling):
    gain = gain_of(coupling, lax.axis_index("orb") * ROWS, ROWS)
    return jnp.concatenate([gain] * ROUNDS, axis=0)


LAST = pl.BlockSpec((1, 1, COLS, WIDE), lambda i: (ROUNDS - 1, TIMES // ROUNDS - 1, 0, 0))


def plain(shape):
    return pl.BlockSpec(shape, lambda i: (0,) * len(shape))


def head_kernel(last, coupling, payload, row):
    row[...] = last[0, 0]
    sigma = self_energy(last[0, 0], own_gain(coupling[...]))
    for z in range(ZS):
        payload[z] = sigma


def head(rows_of, coupling):
    shape = (ZS, COLS, WIDE)
    return pl.pallas_call(
        head_kernel,
        grid=(1,),
        in_specs=[LAST, plain((1, ORB))],
        out_specs=[plain(shape), plain((COLS, WIDE))],
        out_shape=[
            jax.ShapeDtypeStruct(shape, jnp.bfloat16),
            jax.ShapeDtypeStruct((COLS, WIDE), jnp.bfloat16),
        ],
        compiler_params=pltpu.CompilerParams(vmem_limit_bytes=56 * 1024 * 1024),
        name="head",
    )(rows_of, coupling)


def ring_sum(pieces):
    a, b, c, d = pieces
    return (a + c) + (b + d)


def piece_at(pieces, distance, index, slot):
    if distance != 2:
        return pieces[(0, 1, None, 4)[distance]][index, slot]
    near = lax.rem(index, 2)
    return jnp.where(index < 2, pieces[2][near, slot], pieces[3][near, slot])


def collect(place, riders, out):
    x, y = place[3], place[4]
    firsts, (b0, b1, low_two, high_two, b3) = riders[:5], riders[5:]
    source = lax.rem(x + 1, XS)

    def rider(index):
        rows = []
        for i in range(YS):
            at = lax.rem(y - i + YS, YS)
            slab = piece_at(firsts, 0, at, GROUP + index)
            for d in range(1, XS):
                other = piece_at(firsts, d, at, GROUP + index)
                slab = jnp.where(source == d, other, slab)
            rows.append(slab)
        return jnp.concatenate(rows, axis=0)

    newest = joined(rider(0), rider(1))
    corner = stepped(rider(2), hermitian(newest)).astype(jnp.bfloat16)
    for i in range(YS):
        rings = []
        for dy in range(YS):
            if dy == 2:
                halves = (low_two, high_two)
                slabs = [halves[dx // 2][dx % 2, GROUP + i] for dx in range(XS)]
            else:
                piece = (b0, b1, None, b3)[dy]
                slabs = [piece[dx, GROUP + i] for dx in range(XS)]
            rings.append(ring_sum([slab.astype(jnp.float32) for slab in slabs]))
        out[2 * COLS + i * ROWS : 2 * COLS + (i + 1) * ROWS] = ring_sum(rings)
    out[2 * COLS + ORB :] = corner.astype(jnp.float32)


def load_kernel(core, own, other, *refs):
    buffers, arrived = refs[:-1], refs[-1]
    copies = []
    for a in range(ROUNDS):
        rows = pl.ds(a * ROWS, COLS - a * ROWS)
        for side, table in enumerate((own, other)):
            i = a * CORES + side
            copies.append(
                pltpu.make_async_copy(
                    table.at[a, :, :, core[0], rows, :], buffers[i], arrived.at[i]
                )
            )
            copies[-1].start()
    for copy in copies:
        copy.wait()


def load(core, own, other):
    far = pl.BlockSpec(memory_space=pl.ANY)
    counts = [COLS - a * ROWS for a in range(ROUNDS) for _ in range(CORES)]
    return pl.pallas_call(
        load_kernel,
        in_specs=[pl.BlockSpec(memory_space=pltpu.SMEM), far, far],
        out_specs=[pl.BlockSpec(memory_space=pltpu.VMEM)] * len(counts),
        out_shape=[
            jax.ShapeDtypeStruct((XS, ZS, count, WIDE), jnp.bfloat16) for count in counts
        ],
        scratch_shapes=[pltpu.SemaphoreType.DMA((len(counts),))],
        compiler_params=pltpu.CompilerParams(vmem_limit_bytes=47 * 1024 * 1024),
        cost_estimate=pl.CostEstimate(
            flops=0, bytes_accessed=12000000, transcendentals=0
        ),
        name="load",
    )(core, own, other)


PARTS = 1


def collide_kernel(place, *refs):
    buffers, refs = refs[: ROUNDS * CORES], refs[ROUNDS * CORES :]
    pieces, (out, total, factor) = refs[:10], refs[10:]
    firsts, (b0, b1, low_two, high_two, b3) = pieces[:5], pieces[5:]
    core, x, y = place[0], place[3], place[4]
    sources = [lax.rem(x - dx + XS, XS) for dx in range(XS)]
    empty = jnp.zeros((ORB, WIDE), jnp.bfloat16)
    for dy in range(YS):
        row = pl.multiple_of(lax.rem(y - dy + YS, YS) * ROWS, ROWS)
        for dx in range(XS):
            if dy == 2:
                piece = (low_two, high_two)[dx // 2].at[dx % 2]
            else:
                piece = (b0, b1, None, b3)[dy].at[dx]
            for z in range(ZS):
                for r in range(HALF):
                    factor[r, dx * ZS + z, pl.ds(row, ROWS), :] = piece[z * HALF + r]

    for a in range(ROUNDS):
        low, count = a * ROWS, COLS - a * ROWS
        for part in range(PARTS):
            groups = [
                (dx, z)
                for dx in range(part * XS // PARTS, (part + 1) * XS // PARTS)
                for z in range(ZS)
            ]
            sides = []
            for side, target in enumerate((place[1], place[2])):
                table = buffers[a * CORES + side]
                blocks = []
                for dx, z in groups:
                    block = table[sources[dx], z]
                    time = (sources[dx] * ZS + z) * CORES + core
                    diagonal = jnp.where(
                        time <= target, block[:ROWS], jnp.zeros_like(block[:ROWS])
                    )
                    if count > ROWS:
                        diagonal = jnp.concatenate([diagonal, block[ROWS:]], axis=0)
                    blocks.append(diagonal)
                sides.append(jnp.concatenate(blocks, axis=1))
            blocks = []
            for dx, z in groups:
                if a < HALF:
                    block = jnp.concatenate(
                        [
                            piece_at(firsts, dx, lax.rem(y - i + YS, YS), z * HALF + a)
                            for i in range(YS)
                        ],
                        axis=0,
                    )
                else:
                    block = factor[a - HALF, dx * ZS + z]
                blocks.append(jnp.concatenate([block, empty], axis=1))
                blocks.append(jnp.concatenate([empty, block], axis=1))
            product = jnp.dot(
                jnp.concatenate(sides, axis=0),
                jnp.concatenate(blocks, axis=0),
                preferred_element_type=jnp.float32,
            )
            if a == 0 and part == 0:
                total[0], total[1] = product[:count], product[count:]
            else:
                total[0, low:, :] += product[:count]
                total[1, low:, :] += product[count:]

    for side in range(2):
        rows = pl.ds(side * COLS, COLS)
        out[rows, :] = total[side, :, :WIDE] + times_i(total[side, :, WIDE:])
    if pieces[0].shape[1] > GROUP:
        collect(place, pieces, out)


def collide(place, history, first, second):
    pieces = first + second
    riding = first[0].shape[1] > GROUP
    shape = (2 * COLS + (2 * ORB if riding else 0), WIDE)
    whole = pl.BlockSpec(memory_space=pltpu.VMEM)
    return pl.pallas_call(
        collide_kernel,
        in_specs=[pl.BlockSpec(memory_space=pltpu.SMEM)]
        + [whole] * (len(history) + len(pieces)),
        out_specs=whole,
        scratch_shapes=[
            pltpu.VMEM((2, COLS, 2 * WIDE), jnp.float32),
            pltpu.VMEM((HALF, XS * ZS, ORB, WIDE), jnp.bfloat16),
        ],
        out_shape=jax.ShapeDtypeStruct(shape, jnp.float32),
        compiler_params=pltpu.CompilerParams(vmem_limit_bytes=24 * 1024 * 1024),
        name="collide",
    )(place, *history, *pieces)


def pair(value):
    high = value.astype(jnp.bfloat16)
    return high, (value - high.astype(jnp.float32)).astype(jnp.bfloat16)


def joined(high, low):
    return high.astype(jnp.float32) + low.astype(jnp.float32)


def update_kernel(sums, theirs, last, hopping, coupling, row_out, payload):
    older = last[...]
    change = hopped(older, hopping[...]) + STEP * (sums[:COLS] + theirs[...])
    row = stepped(older, change).astype(jnp.bfloat16)
    sigma = self_energy(row, own_gain(coupling[...]))
    row_out[...] = row
    overlap = lax.dot_general(
        row, sigma, (((0,), (0,)), ((), ())), preferred_element_type=jnp.float32
    )
    column = (times_i(overlap[ORB:]) - overlap[:ORB]).astype(jnp.bfloat16)
    riders = pair(change[COLS - ROWS :]) + (older[COLS - ROWS :], column)
    whole = jnp.concatenate((sigma,) + riders, axis=0)
    for z in range(ZS):
        payload[z] = whole


def update(sums, theirs, last, hopping, coupling):
    shapes = [(COLS, WIDE), (ZS, COLS + EXTRA * ROWS + ORB, WIDE)]
    return pl.pallas_call(
        update_kernel,
        out_shape=[jax.ShapeDtypeStruct(shape, jnp.bfloat16) for shape in shapes],
        compiler_params=SMALL,
        name="update",
    )(sums, theirs, last, hopping, coupling)


def close_kernel(sums, theirs, row, hopping, coupling, *refs):
    row_two, corner_one, edge_two, corner_two, lines = refs
    hop = hopping[...]
    on_last = lax.axis_index("core") == 1
    corner = jnp.where(on_last, sums[2 * COLS + ORB :], theirs[COLS + ORB :]).astype(jnp.bfloat16)
    column = sums[2 * COLS : 2 * COLS + ORB] + theirs[COLS : COLS + ORB]
    corner_factor = matrix_of(self_energy(corner, gain_of(coupling[...], 0, ORB)))
    older = row[...]
    change = (
        hopped(older, hop)
        + jnp.dot(older, corner_factor, preferred_element_type=jnp.float32)
        + STEP * (sums[:COLS] + theirs[:COLS])
    )
    row_two[...] = stepped(older, change).astype(jnp.bfloat16)
    edge_change = hopped(corner, hop) + STEP * (
        column + jnp.dot(corner, corner_factor, preferred_element_type=jnp.float32)
    )
    lines[0] = corner.astype(jnp.float32)
    lines[1] = stepped(corner, edge_change)
    lines[2] = stepped(corner, hermitian(edge_change))
    own = pl.ds(pl.multiple_of(lax.axis_index("orb") * ROWS, ROWS), ROWS)
    for i, out in enumerate((corner_one, edge_two, corner_two)):
        out[...] = lines[i, own, :].astype(jnp.bfloat16)


def close(sums, theirs, row, hopping, coupling):
    shapes = [(COLS, WIDE)] + [(ROWS, WIDE)] * 3
    return pl.pallas_call(
        close_kernel,
        out_shape=[jax.ShapeDtypeStruct(shape, jnp.bfloat16) for shape in shapes],
        scratch_shapes=[pltpu.VMEM((3, ORB, WIDE), jnp.float32)],
        compiler_params=SMALL,
        name="close",
    )(sums, theirs, row, hopping, coupling)


def body(history, hopping, coupling):
    x, z = lax.axis_index("x"), lax.axis_index("z")
    core, y = lax.axis_index("core"), lax.axis_index("orb")
    owner = (x * ZS + z) * CORES + core
    place = jnp.stack([core, owner, owner + 1 - 2 * core, x, y]).astype(jnp.int32)
    table = history.reshape(ROUNDS, XS, ZS, CORES, COLS, WIDE)
    rows_of = history.reshape(ROUNDS, TIMES // ROUNDS, COLS, WIDE)
    coupling = coupling.reshape(1, ORB)

    def along_one(first, second):
        first, second = lax.optimization_barrier((first, second))
        first, second = around(first, "orb"), around(second, "x")
        first, second = lax.optimization_barrier(first), lax.optimization_barrier(second)
        first, second = jnp.concatenate(first), jnp.concatenate(second)
        return lax.optimization_barrier(first), lax.optimization_barrier(second)

    def ring(array, axis):
        forward = [(i, (i + 1) % 4) for i in range(4)]
        backward = [(i, (i + 3) % 4) for i in range(4)]
        ahead = lax.ppermute(array, axis, forward)
        behind = lax.ppermute(array, axis, backward)
        middle = array.shape[0] // 2
        low = lax.ppermute(ahead[:middle], axis, forward)
        high = lax.ppermute(behind[middle:], axis, backward)
        return [
            piece.reshape(-1, array.shape[0] // 4, ROWS, WIDE)
            for piece in (array, ahead, low, high, behind)
        ]

    def along_again(first, second):
        return lax.optimization_barrier((ring(first, "x"), ring(second, "orb")))

    def plane_parts(planes):
        parts = planes.reshape(ZS, -1, ROWS, WIDE)
        return (
            parts[:, :HALF].reshape(GROUP, ROWS, WIDE),
            parts[:, HALF:ROUNDS].reshape(GROUP, ROWS, WIDE),
        )

    other = swap_cores(table)
    payload, last_row = head(rows_of, coupling)
    planes = lax.all_to_all(payload, "z", 0, 0)
    planes, other = lax.optimization_barrier((planes, other))
    first, second = along_one(*plane_parts(planes))
    first, own, other, place = lax.optimization_barrier((first, table, other, place))
    history = load(place[:1], own, other)
    first, second = along_again(first, second)
    sums = collide(place, history, first, second)
    row_one, payload = update(sums, swap_cores(sums[COLS:]), last_row, hopping, coupling)

    planes = lax.all_to_all(payload, "z", 0, 0)
    first, second = plane_parts(planes)
    parts = planes.reshape(ZS, -1, ROWS, WIDE)
    riders = parts[ZS - 1, ROUNDS : ROUNDS + EXTRA]
    column = jnp.sum(parts[:, ROUNDS + EXTRA :].astype(jnp.float32), axis=0)
    first, second = along_again(
        *along_one(
            jnp.concatenate([first, riders]),
            jnp.concatenate([second, column.astype(jnp.bfloat16)]),
        )
    )
    sums = collide(place, history, first, second)
    row_two, corner_one, edge_two, corner_two = close(
        sums, swap_cores(sums[COLS:]), row_one, hopping, coupling
    )
    shape = (ROUNDS, 1, ROWS, WIDE)
    return (row_one.reshape(shape), corner_one, row_two.reshape(shape), edge_two, corner_two)


def solution(mesh):
    fine = Mesh(mesh.devices.reshape(XS, ZS, CORES, YS), ("x", "z", "core", "orb"))
    tm = ("x", "z", "core")
    return jax.shard_map(
        body,
        mesh=fine,
        in_specs=(P(None, None, None, tm, "orb", None), P(), P()),
        out_specs=(
            P(None, tm, "orb", None),
            P("orb", None),
            P(None, tm, "orb", None),
            P("orb", None),
            P("orb", None),
        ),
        check_vma=False,
    )
```

```python
import jax
import jax.numpy as jnp
from jax import lax
from jax.experimental import pallas as pl
from jax.experimental.pallas import tpu as pltpu
from jax.sharding import Mesh, PartitionSpec as P

STEP = 0.08
XS, ZS, CORES, YS = 4, 8, 2, 4
ROUNDS = 6
ORB = 64
ROWS = ORB // YS
WIDE = 2 * ORB
COLS = ROUNDS * ROWS
TIMES = ROUNDS * XS * ZS * CORES
EXTRA = 3
HALF = ROUNDS // 2
GROUP = ZS * HALF
SMALL = pltpu.CompilerParams(vmem_limit_bytes=8 * 1024 * 1024)


def swap_cores(array):
    return lax.ppermute(array, "core", [(0, 1), (1, 0)])


def around(array, axis):
    pieces = {0: array}
    for distance in (1, 3, 2):
        pairs = [(i, (i + distance) % 4) for i in range(4)]
        pieces[distance] = lax.ppermute(array, axis, pairs)
    return [pieces[d] for d in range(4)]


def halves_swapped(value):
    return jnp.concatenate([value[:, ORB:], value[:, :ORB]], axis=-1)


def times_i(value):
    return jnp.concatenate([-value[:, ORB:], value[:, :ORB]], axis=-1)


def matrix_of(value):
    return jnp.concatenate([value, times_i(value)], axis=0)


def stepped(older, change):
    return older.astype(jnp.float32) - STEP * times_i(change)


def self_energy(blocks, gain):
    parts = blocks.astype(jnp.float32)
    square = parts * parts
    return (gain * (square + halves_swapped(square)) * parts).astype(jnp.bfloat16)


def hermitian(whole):
    real_part = whole[:, :ORB]
    imag_part = whole[:, ORB:]
    return jnp.concatenate([real_part + real_part.T, imag_part - imag_part.T], axis=-1)


def gain_of(row, first, count):
    lane = lax.broadcasted_iota(jnp.int32, (count, ORB), 1)
    line = lax.broadcasted_iota(jnp.int32, (count, ORB), 0)
    mine = jnp.where(lane == line + first, jnp.broadcast_to(row, (count, ORB)), 0.0)
    column = jnp.sum(mine, axis=1, keepdims=True)
    return -(column * jnp.concatenate([row, row], axis=1))


def hopped(blocks, hopping):
    empty = jnp.zeros_like(hopping)
    both = jnp.concatenate(
        [
            jnp.concatenate([hopping, empty], axis=1),
            jnp.concatenate([empty, hopping], axis=1),
        ],
        axis=0,
    )
    return lax.dot_general(
        blocks, both, (((1,), (1,)), ((), ())), preferred_element_type=jnp.float32
    )


def own_gain(coupling):
    gain = gain_of(coupling, lax.axis_index("orb") * ROWS, ROWS)
    return jnp.concatenate([gain] * ROUNDS, axis=0)


LAST = pl.BlockSpec((1, 1, COLS, WIDE), lambda i: (ROUNDS - 1, TIMES // ROUNDS - 1, 0, 0))


def plain(shape):
    return pl.BlockSpec(shape, lambda i: (0,) * len(shape))


def head_kernel(last, coupling, payload, row):
    row[...] = last[0, 0]
    sigma = self_energy(last[0, 0], own_gain(coupling[...]))
    for z in range(ZS):
        payload[z] = sigma


def head(rows_of, coupling):
    shape = (ZS, COLS, WIDE)
    return pl.pallas_call(
        head_kernel,
        grid=(1,),
        in_specs=[LAST, plain((1, ORB))],
        out_specs=[plain(shape), plain((COLS, WIDE))],
        out_shape=[
            jax.ShapeDtypeStruct(shape, jnp.bfloat16),
            jax.ShapeDtypeStruct((COLS, WIDE), jnp.bfloat16),
        ],
        compiler_params=pltpu.CompilerParams(vmem_limit_bytes=56 * 1024 * 1024),
        name="head",
    )(rows_of, coupling)


def ring_sum(pieces):
    a, b, c, d = pieces
    return (a + c) + (b + d)


def piece_at(pieces, distance, index, slot):
    if distance != 2:
        return pieces[(0, 1, None, 4)[distance]][index, slot]
    near = lax.rem(index, 2)
    return jnp.where(index < 2, pieces[2][near, slot], pieces[3][near, slot])


def collect(place, riders, out):
    x, y = place[3], place[4]
    firsts, (b0, b1, low_two, high_two, b3) = riders[:5], riders[5:]
    source = lax.rem(x + 1, XS)

    def rider(index):
        rows = []
        for i in range(YS):
            at = lax.rem(y - i + YS, YS)
            slab = piece_at(firsts, 0, at, GROUP + index)
            for d in range(1, XS):
                other = piece_at(firsts, d, at, GROUP + index)
                slab = jnp.where(source == d, other, slab)
            rows.append(slab)
        return jnp.concatenate(rows, axis=0)

    newest = joined(rider(0), rider(1))
    corner = stepped(rider(2), hermitian(newest)).astype(jnp.bfloat16)
    for i in range(YS):
        rings = []
        for dy in range(YS):
            if dy == 2:
                halves = (low_two, high_two)
                slabs = [halves[dx // 2][dx % 2, GROUP + i] for dx in range(XS)]
            else:
                piece = (b0, b1, None, b3)[dy]
                slabs = [piece[dx, GROUP + i] for dx in range(XS)]
            rings.append(ring_sum([slab.astype(jnp.float32) for slab in slabs]))
        out[2 * COLS + i * ROWS : 2 * COLS + (i + 1) * ROWS] = ring_sum(rings)
    out[2 * COLS + ORB :] = corner.astype(jnp.float32)


def load_kernel(core, own, other, *refs):
    buffers, arrived = refs[:-1], refs[-1]
    copies = []
    for a in range(ROUNDS):
        rows = pl.ds(a * ROWS, COLS - a * ROWS)
        for side, table in enumerate((own, other)):
            i = a * CORES + side
            copies.append(
                pltpu.make_async_copy(
                    table.at[a, :, :, core[0], rows, :], buffers[i], arrived.at[i]
                )
            )
            copies[-1].start()
    for copy in copies:
        copy.wait()


def load(core, own, other):
    far = pl.BlockSpec(memory_space=pl.ANY)
    counts = [COLS - a * ROWS for a in range(ROUNDS) for _ in range(CORES)]
    return pl.pallas_call(
        load_kernel,
        in_specs=[pl.BlockSpec(memory_space=pltpu.SMEM), far, far],
        out_specs=[pl.BlockSpec(memory_space=pltpu.VMEM)] * len(counts),
        out_shape=[
            jax.ShapeDtypeStruct((XS, ZS, count, WIDE), jnp.bfloat16) for count in counts
        ],
        scratch_shapes=[pltpu.SemaphoreType.DMA((len(counts),))],
        compiler_params=pltpu.CompilerParams(vmem_limit_bytes=47 * 1024 * 1024),
        cost_estimate=pl.CostEstimate(
            flops=0, bytes_accessed=12000000, transcendentals=0
        ),
        name="load",
    )(core, own, other)


PARTS = 1


def collide_kernel(place, *refs):
    buffers, refs = refs[: ROUNDS * CORES], refs[ROUNDS * CORES :]
    pieces, (out, total, factor) = refs[:10], refs[10:]
    firsts, (b0, b1, low_two, high_two, b3) = pieces[:5], pieces[5:]
    core, x, y = place[0], place[3], place[4]
    sources = [lax.rem(x - dx + XS, XS) for dx in range(XS)]
    empty = jnp.zeros((ORB, WIDE), jnp.bfloat16)
    for dy in range(YS):
        row = pl.multiple_of(lax.rem(y - dy + YS, YS) * ROWS, ROWS)
        for dx in range(XS):
            if dy == 2:
                piece = (low_two, high_two)[dx // 2].at[dx % 2]
            else:
                piece = (b0, b1, None, b3)[dy].at[dx]
            for z in range(ZS):
                for r in range(HALF):
                    factor[r, dx * ZS + z, pl.ds(row, ROWS), :] = piece[z * HALF + r]

    for a in range(ROUNDS):
        low, count = a * ROWS, COLS - a * ROWS
        for part in range(PARTS):
            groups = [
                (dx, z)
                for dx in range(part * XS // PARTS, (part + 1) * XS // PARTS)
                for z in range(ZS)
            ]
            sides = []
            for side, target in enumerate((place[1], place[2])):
                table = buffers[a * CORES + side]
                blocks = []
                for dx, z in groups:
                    block = table[sources[dx], z]
                    time = (sources[dx] * ZS + z) * CORES + core
                    diagonal = jnp.where(
                        time <= target, block[:ROWS], jnp.zeros_like(block[:ROWS])
                    )
                    if count > ROWS:
                        diagonal = jnp.concatenate([diagonal, block[ROWS:]], axis=0)
                    blocks.append(diagonal)
                sides.append(jnp.concatenate(blocks, axis=1))
            blocks = []
            for dx, z in groups:
                if a < HALF:
                    block = jnp.concatenate(
                        [
                            piece_at(firsts, dx, lax.rem(y - i + YS, YS), z * HALF + a)
                            for i in range(YS)
                        ],
                        axis=0,
                    )
                else:
                    block = factor[a - HALF, dx * ZS + z]
                blocks.append(jnp.concatenate([block, empty], axis=1))
                blocks.append(jnp.concatenate([empty, block], axis=1))
            product = jnp.dot(
                jnp.concatenate(sides, axis=0),
                jnp.concatenate(blocks, axis=0),
                preferred_element_type=jnp.float32,
            )
            if a == 0 and part == 0:
                total[0], total[1] = product[:count], product[count:]
            else:
                total[0, low:, :] += product[:count]
                total[1, low:, :] += product[count:]

    for side in range(2):
        rows = pl.ds(side * COLS, COLS)
        out[rows, :] = total[side, :, :WIDE] + times_i(total[side, :, WIDE:])
    if pieces[0].shape[1] > GROUP:
        collect(place, pieces, out)


def collide(place, history, first, second):
    pieces = first + second
    riding = first[0].shape[1] > GROUP
    shape = (2 * COLS + (2 * ORB if riding else 0), WIDE)
    whole = pl.BlockSpec(memory_space=pltpu.VMEM)
    return pl.pallas_call(
        collide_kernel,
        in_specs=[pl.BlockSpec(memory_space=pltpu.SMEM)]
        + [whole] * (len(history) + len(pieces)),
        out_specs=whole,
        scratch_shapes=[
            pltpu.VMEM((2, COLS, 2 * WIDE), jnp.float32),
            pltpu.VMEM((HALF, XS * ZS, ORB, WIDE), jnp.bfloat16),
        ],
        out_shape=jax.ShapeDtypeStruct(shape, jnp.float32),
        compiler_params=pltpu.CompilerParams(vmem_limit_bytes=24 * 1024 * 1024),
        name="collide",
    )(place, *history, *pieces)


def pair(value):
    high = value.astype(jnp.bfloat16)
    return high, (value - high.astype(jnp.float32)).astype(jnp.bfloat16)


def joined(high, low):
    return high.astype(jnp.float32) + low.astype(jnp.float32)


def update_kernel(sums, theirs, last, hopping, coupling, row_out, payload):
    older = last[...]
    change = hopped(older, hopping[...]) + STEP * (sums[:COLS] + theirs[...])
    row = stepped(older, change).astype(jnp.bfloat16)
    sigma = self_energy(row, own_gain(coupling[...]))
    row_out[...] = row
    overlap = lax.dot_general(
        row, sigma, (((0,), (0,)), ((), ())), preferred_element_type=jnp.float32
    )
    column = (times_i(overlap[ORB:]) - overlap[:ORB]).astype(jnp.bfloat16)
    riders = pair(change[COLS - ROWS :]) + (older[COLS - ROWS :], column)
    whole = jnp.concatenate((sigma,) + riders, axis=0)
    for z in range(ZS):
        payload[z] = whole


def update(sums, theirs, last, hopping, coupling):
    shapes = [(COLS, WIDE), (ZS, COLS + EXTRA * ROWS + ORB, WIDE)]
    return pl.pallas_call(
        update_kernel,
        out_shape=[jax.ShapeDtypeStruct(shape, jnp.bfloat16) for shape in shapes],
        compiler_params=SMALL,
        name="update",
    )(sums, theirs, last, hopping, coupling)


def close_kernel(sums, theirs, row, hopping, coupling, *refs):
    row_two, corner_one, edge_two, corner_two, lines = refs
    hop = hopping[...]
    on_last = lax.axis_index("core") == 1
    corner = jnp.where(on_last, sums[2 * COLS + ORB :], theirs[COLS + ORB :]).astype(jnp.bfloat16)
    column = sums[2 * COLS : 2 * COLS + ORB] + theirs[COLS : COLS + ORB]
    corner_factor = matrix_of(self_energy(corner, gain_of(coupling[...], 0, ORB)))
    older = row[...]
    change = (
        hopped(older, hop)
        + jnp.dot(older, corner_factor, preferred_element_type=jnp.float32)
        + STEP * (sums[:COLS] + theirs[:COLS])
    )
    row_two[...] = stepped(older, change).astype(jnp.bfloat16)
    edge_change = hopped(corner, hop) + STEP * (
        column + jnp.dot(corner, corner_factor, preferred_element_type=jnp.float32)
    )
    lines[0] = corner.astype(jnp.float32)
    lines[1] = stepped(corner, edge_change)
    lines[2] = stepped(corner, hermitian(edge_change))
    own = pl.ds(pl.multiple_of(lax.axis_index("orb") * ROWS, ROWS), ROWS)
    for i, out in enumerate((corner_one, edge_two, corner_two)):
        out[...] = lines[i, own, :].astype(jnp.bfloat16)


def close(sums, theirs, row, hopping, coupling):
    shapes = [(COLS, WIDE)] + [(ROWS, WIDE)] * 3
    return pl.pallas_call(
        close_kernel,
        out_shape=[jax.ShapeDtypeStruct(shape, jnp.bfloat16) for shape in shapes],
        scratch_shapes=[pltpu.VMEM((3, ORB, WIDE), jnp.float32)],
        compiler_params=SMALL,
        name="close",
    )(sums, theirs, row, hopping, coupling)


def body(history, hopping, coupling):
    x, z = lax.axis_index("x"), lax.axis_index("z")
    core, y = lax.axis_index("core"), lax.axis_index("orb")
    owner = (x * ZS + z) * CORES + core
    place = jnp.stack([core, owner, owner + 1 - 2 * core, x, y]).astype(jnp.int32)
    table = history.reshape(ROUNDS, XS, ZS, CORES, COLS, WIDE)
    rows_of = history.reshape(ROUNDS, TIMES // ROUNDS, COLS, WIDE)
    coupling = coupling.reshape(1, ORB)

    def along_one(first, second):
        first, second = lax.optimization_barrier((first, second))
        first, second = around(first, "orb"), around(second, "x")
        first, second = lax.optimization_barrier(first), lax.optimization_barrier(second)
        first, second = jnp.concatenate(first), jnp.concatenate(second)
        return lax.optimization_barrier(first), lax.optimization_barrier(second)

    def ring(array, axis):
        forward = [(i, (i + 1) % 4) for i in range(4)]
        backward = [(i, (i + 3) % 4) for i in range(4)]
        ahead = lax.ppermute(array, axis, forward)
        behind = lax.ppermute(array, axis, backward)
        middle = array.shape[0] // 2
        low = lax.ppermute(ahead[:middle], axis, forward)
        high = lax.ppermute(behind[middle:], axis, backward)
        return [
            piece.reshape(-1, array.shape[0] // 4, ROWS, WIDE)
            for piece in (array, ahead, low, high, behind)
        ]

    def along_again(first, second):
        return lax.optimization_barrier((ring(first, "x"), ring(second, "orb")))

    def plane_parts(planes):
        parts = planes.reshape(ZS, -1, ROWS, WIDE)
        return (
            parts[:, :HALF].reshape(GROUP, ROWS, WIDE),
            parts[:, HALF:ROUNDS].reshape(GROUP, ROWS, WIDE),
        )

    other = swap_cores(table)
    payload, last_row = head(rows_of, coupling)
    planes = lax.all_to_all(payload, "z", 0, 0)
    first, second = along_one(*plane_parts(planes))
    first, own, other, place = lax.optimization_barrier((first, table, other, place))
    history = load(place[:1], own, other)
    first, second = along_again(first, second)
    sums = collide(place, history, first, second)
    row_one, payload = update(sums, swap_cores(sums[COLS:]), last_row, hopping, coupling)

    planes = lax.all_to_all(payload, "z", 0, 0)
    first, second = plane_parts(planes)
    parts = planes.reshape(ZS, -1, ROWS, WIDE)
    riders = parts[ZS - 1, ROUNDS : ROUNDS + EXTRA]
    column = jnp.sum(parts[:, ROUNDS + EXTRA :].astype(jnp.float32), axis=0)
    first, second = along_again(
        *along_one(
            jnp.concatenate([first, riders]),
            jnp.concatenate([second, column.astype(jnp.bfloat16)]),
        )
    )
    sums = collide(place, history, first, second)
    row_two, corner_one, edge_two, corner_two = close(
        sums, swap_cores(sums[COLS:]), row_one, hopping, coupling
    )
    shape = (ROUNDS, 1, ROWS, WIDE)
    return (row_one.reshape(shape), corner_one, row_two.reshape(shape), edge_two, corner_two)


def solution(mesh):
    fine = Mesh(mesh.devices.reshape(XS, ZS, CORES, YS), ("x", "z", "core", "orb"))
    tm = ("x", "z", "core")
    return jax.shard_map(
        body,
        mesh=fine,
        in_specs=(P(None, None, None, tm, "orb", None), P(), P()),
        out_specs=(
            P(None, tm, "orb", None),
            P("orb", None),
            P(None, tm, "orb", None),
            P("orb", None),
            P("orb", None),
        ),
        check_vma=False,
    )
```
